128 devices in a mesh: dp: 16 (over y_lo, x, core), tensor: 8 (over y_hi, z).
Axes of the slice: x: 4, y: 4 (y_hi: 2, y_lo: 2; y = y_hi * 2 + y_lo), z: 4, core: 2. Of those that a mesh axis runs over, the one named last changes fastest.
Arguments:
- inputs: bfloat16 [512, 8192], P('tensor', 'dp'), may hold values from -6 to 6
- ordering: int32 [512], replicated, may hold values from 0 to 511, each once
- cotangent: float32 [512], P(('dp', 'tensor')), may hold values from -192 to 192
- gate_weight: bfloat16 [8192, 14336], P('dp', 'tensor'), may hold values from -0.0625 to 0.0625
- up_weight: bfloat16 [8192, 14336], P('dp', 'tensor'), may hold values from -0.0625 to 0.0625
- down_weight: bfloat16 [14336, 8192], P('tensor', 'dp'), may hold values from -0.046875 to 0.046875
- value_head: bfloat16 [8192], P('dp'), may hold values from -0.0625 to 0.0625
Outputs:
- scores: float32 [512], P('tensor')
- input_grad: bfloat16 [512, 8192], P(('dp', 'tensor'))
- gate_grad: bfloat16 [8192, 14336], P('dp', 'tensor')
- up_grad: bfloat16 [8192, 14336], P('dp', 'tensor')
- down_grad: bfloat16 [14336, 8192], P('tensor', 'dp')
The draws below stay inside these ranges and needn't reach their ends.
Inputs may be any that keep to these rules, and one draw needn't show every extreme that they name: `ordering`: each token index appears exactly once.
All inputs are finite; a program needn't handle non-finite values.
Results may differ from the reference program's by a relative error of at most 0.01.
Values may be sent and summed in bfloat16 or wider, within the bound.
A program may use at most 128 MiB of HBM per device.

```python
import jax
import jax.numpy as jnp
from jax import lax

D = 8192
FF = 14336
TOKENS = 512


def shard_levels(own_key, shape, cuts, smallest, top_value):
    def one(dim, blocks):
        draws = jax.random.uniform(jax.random.fold_in(jax.random.fold_in(own_key, 6), dim), (blocks,), jnp.float32, smallest / len(cuts), top_value / len(cuts))
        return jnp.repeat(jnp.exp(draws), shape[dim] // blocks).reshape((-1,) + (1,) * (len(shape) - dim - 1))

    loudness = one(*cuts[0])
    for cut in cuts[1:]:
        loudness = loudness * one(*cut)
    return loudness


def bell_draw(key, shape, scale, reach, cuts=(), held_as=jnp.bfloat16):
    level = shard_levels(key, shape, cuts, -0.22, 0.18) if cuts else 1.0
    values = jax.random.normal(key, shape, jnp.float32) * scale * level
    return jnp.minimum(jnp.maximum(values, -reach), reach).astype(held_as)


def setup_inputs(seed: int = 0) -> dict:
    splits = jax.random.split(jax.random.key(seed), 8)
    inputs = bell_draw(splits[0], (TOKENS, D), 1.0, 6.0, ((0, 8), (1, 16)))
    ordering = jax.random.permutation(splits[1], TOKENS).astype(jnp.int32)
    cotangent = bell_draw(splits[2], (TOKENS,), 32.0, 192.0, ((0, 128),), jnp.float32)
    gate_weight = bell_draw(splits[3], (D, FF), D ** -0.5, 0.0625, ((0, 16), (1, 8)))
    up_weight = bell_draw(splits[4], (D, FF), D ** -0.5, 0.0625, ((0, 16), (1, 8)))
    down_weight = bell_draw(splits[5], (FF, D), FF ** -0.5, 0.046875, ((0, 8), (1, 16)))
    value_head = bell_draw(splits[6], (D,), D ** -0.5, 0.0625, ((0, 16),))
    return {"inputs": inputs, "ordering": ordering, "cotangent": cotangent, "gate_weight": gate_weight, "up_weight": up_weight, "down_weight": down_weight, "value_head": value_head}


def activate(gate, up):
    return (gate * jax.nn.sigmoid(gate) * up).astype(jnp.bfloat16)


def unit_grads(gate, up, unit_back):
    sigmoid_part = jax.nn.sigmoid(gate)
    swish = gate * sigmoid_part
    hidden = (swish * up).astype(jnp.bfloat16)
    gate_low = (unit_back * up * sigmoid_part * (1.0 + gate * (1.0 - sigmoid_part))).astype(jnp.bfloat16)
    up_low = (unit_back * swish).astype(jnp.bfloat16)
    return hidden, gate_low, up_low


def contract_rows(left, right):
    return lax.dot_general(left, right, (((0,), (0,)), ((), ())), preferred_element_type=jnp.float32)


def contract_cols(left, right):
    return lax.dot_general(left, right, (((1,), (1,)), ((), ())), preferred_element_type=jnp.float32)


def reference(inputs, ordering, cotangent, gate_weight, up_weight, down_weight, value_head):
    gate_serve = jnp.dot(inputs, gate_weight, preferred_element_type=jnp.float32)
    up_serve = jnp.dot(inputs, up_weight, preferred_element_type=jnp.float32)
    hidden_serve = activate(gate_serve, up_serve)
    lifted = jnp.dot(hidden_serve, down_weight, preferred_element_type=jnp.float32)
    head_float = value_head.astype(jnp.float32)
    scores = jnp.sum((inputs.astype(jnp.float32) + lifted) * head_float[None, :], axis=1)
    relayed = jnp.take(inputs, ordering.astype(jnp.int32), axis=0)
    gate_train = jnp.dot(relayed, gate_weight, preferred_element_type=jnp.float32)
    up_train = jnp.dot(relayed, up_weight, preferred_element_type=jnp.float32)
    out_grad = cotangent.astype(jnp.float32)[:, None] * head_float[None, :]
    out_low = out_grad.astype(jnp.bfloat16)
    unit_back = contract_cols(out_low, down_weight)
    hidden_train, gate_low, up_low = unit_grads(gate_train, up_train, unit_back)
    down_grad = contract_rows(hidden_train, out_low).astype(jnp.bfloat16)
    gate_grad = contract_rows(relayed, gate_low).astype(jnp.bfloat16)
    up_grad = contract_rows(relayed, up_low).astype(jnp.bfloat16)
    input_grad = (out_grad + contract_cols(gate_low, gate_weight) + contract_cols(up_low, up_weight)).astype(jnp.bfloat16)
    return scores, input_grad, gate_grad, up_grad, down_grad
```

```python
import jax
import jax.numpy as jnp
from jax import lax
from jax.sharding import PartitionSpec as P


def per_device(inputs, ordering, cotangent, gate_weight, up_weight, down_weight, value_head):
    dp_count = lax.axis_size("dp")
    tp_count = lax.axis_size("tensor")
    dp_place = lax.axis_index("dp")
    tp_place = lax.axis_index("tensor")
    head = value_head.astype(jnp.float32)
    columns = lax.all_gather(inputs, "tensor", axis=0, tiled=True)
    tokens = columns.shape[0]
    units = gate_weight.shape[1]
    rows = tokens // dp_count
    both_weight = jnp.concatenate([gate_weight, up_weight], axis=1)
    both = jnp.dot(columns, both_weight, preferred_element_type=jnp.float32).astype(jnp.bfloat16)
    both = lax.psum_scatter(both, "dp", scatter_dimension=0, tiled=True).astype(jnp.float32)
    gate, up = both[:, :units], both[:, units:]
    unit_head = lax.psum(jnp.sum(down_weight.astype(jnp.float32) * head[None, :], axis=1), "dp")
    cot_train = lax.all_gather(cotangent, ("dp", "tensor"), axis=0, tiled=True)
    place = (ordering[:, None] == jnp.arange(tokens)[None, :]).astype(jnp.float32)
    cot_serve = jnp.sum(place * cot_train[:, None], axis=0)
    cot = lax.dynamic_slice_in_dim(cot_serve, dp_place * rows, rows, 0)
    sig = jax.nn.sigmoid(gate)
    swish = gate * sig
    hidden = (swish * up).astype(jnp.bfloat16).astype(jnp.float32)
    back = cot[:, None] * unit_head[None, :]
    gate_low = (back * up * sig * (1.0 + gate * (1.0 - sig))).astype(jnp.bfloat16)
    up_low = (back * swish).astype(jnp.bfloat16)
    low = lax.all_gather(jnp.concatenate([gate_low, up_low], axis=1), "dp", axis=0, tiled=True)
    down_vec = lax.psum(jnp.sum(hidden * cot[:, None], axis=0), "dp")
    down_grad = (down_vec[:, None] * head[None, :]).astype(jnp.bfloat16)
    score = jnp.zeros((tokens,), jnp.float32)
    score = lax.dynamic_update_slice_in_dim(
        score, jnp.sum(inputs.astype(jnp.float32) * head[None, :], axis=1), tp_place * inputs.shape[0], 0
    )
    score = score + lax.dynamic_update_slice_in_dim(
        jnp.zeros((tokens,), jnp.float32), jnp.sum(hidden * unit_head[None, :], axis=1), dp_place * rows, 0
    )
    score = lax.psum(score, ("dp", "tensor"))
    scores = lax.dynamic_slice_in_dim(score, tp_place * inputs.shape[0], inputs.shape[0], 0)
    grads = lax.dot_general(
        columns, low, (((0,), (0,)), ((), ())), preferred_element_type=jnp.float32
    ).astype(jnp.bfloat16)
    gate_grad, up_grad = grads[:, :units], grads[:, units:]
    part = lax.dot_general(
        low, both_weight, (((1,), (1,)), ((), ())), preferred_element_type=jnp.float32
    ).astype(jnp.bfloat16)
    each = tokens // (dp_count * tp_count)

    def layout(values):
        return values.reshape(dp_count, tp_count, each).transpose(1, 0, 2).reshape(tokens)

    part = jnp.take(part, layout(ordering), axis=0)
    summed = lax.psum_scatter(part, "tensor", scatter_dimension=0, tiled=True).astype(jnp.float32)
    band = tokens // tp_count
    cot_band = lax.dynamic_slice_in_dim(layout(cot_train), tp_place * band, band, 0)
    input_rows = (summed + cot_band[:, None] * head[None, :]).astype(jnp.bfloat16)
    input_grad = lax.all_to_all(input_rows, "dp", split_axis=0, concat_axis=1, tiled=True)
    return (scores, input_grad, gate_grad, up_grad, down_grad)


def solution(mesh):
    placed = (
        P("tensor", "dp"),
        P(),
        P(("dp", "tensor")),
        P("dp", "tensor"),
        P("dp", "tensor"),
        P("tensor", "dp"),
        P("dp"),
    )
    return jax.shard_map(
        per_device,
        mesh=mesh,
        in_specs=placed,
        out_specs=(
            P("tensor"),
            P(("dp", "tensor"), None),
            P("dp", "tensor"),
            P("dp", "tensor"),
            P("tensor", "dp"),
        ),
        check_vma=False,
    )
```

```python
import functools

import jax
import jax.numpy as jnp
from jax import lax
from jax.experimental import pallas as pl
from jax.experimental.pallas import tpu as pltpu
from jax.sharding import PartitionSpec as P

BF = jnp.bfloat16
F32 = jnp.float32
MESH = pl.DeviceIdType.MESH
HALF = 896
CUTS = (0, 640, 1280, 1792)
BLOCKS = 8
ROWS = 64


def slot(part, block):
    bits = [(block >> d) & 1 for d in range(3)]
    return 4 * bits[part] + 2 * bits[(part + 1) % 3] + bits[(part + 2) % 3]


def col_tiles(part):
    lo, hi = CUTS[part], CUTS[part + 1]
    return [(c, min(c + 256, hi)) for c in range(lo, hi, 256)]


def dot(a, b):
    return jnp.dot(a, b, preferred_element_type=F32)


def dot_t(a, b):
    return lax.dot_general(a, b, (((1,), (1,)), ((), ())), preferred_element_type=F32)


def kernel(
    x_in, order_col, order_tile, cot_in, head_in, gate_w, up_w, down_w,
    gate_out, up_out, vec_out, score_out, rows_out,
    xs, xt, wb, down_v, place, rs0, rs1, rs2, rb0, rb1, rb2, lb0, lb1, lb2,
    cot_got, a_send, a_got, sums, b_send, b_got, z_send, z_got, z_perm, t_got, s_send, s_got,
    g_sib, g_own, d_send, d_got,
    x_s, x_r, cot_s, cot_r, xf_s, xf_r, w_s, w_r, loc, rs_s, rs_r, a_s, a_r, ag_s, ag_r, b_s, b_r,
    z_s, z_r, t_s, t_r, sc_s, sc_r, g_s, g_r, d_s, d_r,
):
    rsb, rbb, lbb = (rs0, rs1, rs2), (rb0, rb1, rb2), (lb0, lb1, lb2)
    i = lax.axis_index("dp")
    j = lax.axis_index("tensor")
    core = i % 2
    x = (i // 2) % 4
    y = i // 8
    bits = (((x + 1) // 2) % 2, x // 2, y)
    block = bits[0] + 2 * bits[1] + 4 * bits[2]
    sib = (i + 1 - 2 * core, j)
    near = (
        (y * 8 + (x + 1 - 2 * (x % 2)) * 2 + core, j),
        (y * 8 + (3 - x) * 2 + core, j),
        ((1 - y) * 8 + x * 2 + core, j),
    )

    def xor(v, k, width):
        out = 0
        for b in range(width):
            bit = (v // (1 << b)) % 2
            out = out + ((1 - bit) if (k >> b) & 1 else bit) * (1 << b)
        return out

    t_peer = [None] + [(i, xor(j, k, 3)) for k in range(1, 8)]
    d_peer = [None] + [(xor(i, k, 4), j) for k in range(1, 16)]

    def remote(src, dst, send, recv, device):
        return pltpu.make_async_remote_copy(
            src_ref=src, dst_ref=dst, send_sem=send, recv_sem=recv, device_id=device, device_id_type=MESH
        )

    mine = pl.ds(pl.multiple_of(core * HALF, 128), HALF)
    other = pl.ds(pl.multiple_of((1 - core) * HALF, 128), HALF)

    barrier = pltpu.get_barrier_semaphore()
    for device in t_peer[1:] + d_peer[1:]:
        pl.semaphore_signal(barrier, inc=1, device_id=device, device_id_type=MESH)
    local = [
        pltpu.make_async_copy(down_w, down_v, loc.at[0]),
        pltpu.make_async_copy(gate_w.at[:, mine], wb.at[0, :, pl.ds(0, HALF)], loc.at[1]),
        pltpu.make_async_copy(up_w.at[:, mine], wb.at[0, :, pl.ds(HALF, HALF)], loc.at[2]),
    ]
    for copy in local:
        copy.start()
    head_rows = jnp.broadcast_to(head_in[...], (16, 512))
    x_head = dot_t(head_rows, x_in[...])
    xs[0, pl.ds(j, 1)] = x_in[...][None]
    local[0].wait()
    a_send[...] = jnp.zeros_like(a_send)
    a_send[0, 0:1, :] = dot_t(head_rows, down_v[mine, :])[0:1]
    a_send[1, 0:1, :] = dot_t(head_rows, down_v[other, :])[0:1]
    for v in range(2):
        a_send[v, 1:2, 0:ROWS] = x_head[0:1]
    place[...] = (order_col[...] == lax.broadcasted_iota(jnp.int32, (512, 512), 1)).astype(BF)
    pl.semaphore_wait(barrier, 22)

    x_copies = [None]
    cot_copies = [None]
    for k in range(1, 8):
        x_copies.append(remote(x_in, xs.at[0, j], x_s.at[k - 1], x_r.at[k - 1], t_peer[k]))
        x_copies[k].start()
    for k in range(1, 8):
        cot_copies.append(remote(cot_in, cot_got.at[k - 1], cot_s.at[k - 1], cot_r.at[k - 1], t_peer[k]))
        cot_copies[k].start()
    w_copies = [
        remote(gate_w.at[:, other], wb.at[1, :, pl.ds(0, HALF)], w_s.at[0], w_r.at[0], sib),
        remote(up_w.at[:, other], wb.at[1, :, pl.ds(HALF, HALF)], w_s.at[1], w_r.at[1], sib),
    ]
    forward = [remote(x_in, xs.at[1, j], xf_s.at[0], xf_r.at[0], sib)]
    forward[0].start()
    for copy in w_copies:
        copy.start()
    for k in range(1, 8):
        x_copies[k].wait_recv()
        there = xor(j, k, 3)
        forward.append(remote(xs.at[0, there], xs.at[1, there], xf_s.at[k], xf_r.at[k], sib))
        forward[k].start()
    for k in range(1, 8):
        cot_copies[k].wait_recv()
    cot_part = cot_in[...]
    for k in range(7):
        cot_part = cot_part + cot_got[k]
    for v in range(2):
        a_send[v, 4:8, 0:128] = cot_part[0:4]
    a_copies = [remote(a_send.at[1], a_got.at[0], a_s.at[0], a_r.at[0], sib)]
    a_copies[0].start()
    for copy in local[1:]:
        copy.wait()
    for copy in w_copies:
        copy.wait_recv()
    for copy in forward:
        copy.wait_recv()

    rs_copies = {}

    def rs_start(p, s):
        b0, b1, b2 = bits[p], bits[(p + 1) % 3], bits[(p + 2) % 3]
        first, count, land = (
            (4 * (1 - b0), 4, 0), (4 * b0 + 2 * (1 - b1), 2, 4), (4 * b0 + 2 * b1 + 1 - b2, 1, 6),
        )[s]
        rs_copies[p, s] = remote(
            rsb[p].at[pl.ds(first, count)], rbb[p].at[pl.ds(land, count)],
            rs_s.at[3 * p + s], rs_r.at[3 * p + s], near[(p + s) % 3],
        )
        rs_copies[p, s].start()

    x_own = xs[0].reshape(512, 512)
    x_sib = xs[1].reshape(512, 512)
    for p in range(3):
        for lo, hi in col_tiles(p):
            part = (dot(x_own, wb[0, :, lo:hi]) + dot(x_sib, wb[1, :, lo:hi])).astype(BF)
            for blk in range(BLOCKS):
                rsb[p][slot(p, blk), :, lo - CUTS[p]:hi - CUTS[p]] = part[blk * ROWS:(blk + 1) * ROWS]
        rs_start(p, 0)

    a_copies[0].wait()
    a_send[2] = a_send[0] + a_got[0]
    a_copies.append(remote(a_send.at[2], a_got.at[1], a_s.at[1], a_r.at[1], near[0]))
    a_copies[1].start()

    for v in range(2):
        for c in range(0, 512, 128):
            xt[v, c:c + 128, :] = xs[v, :, :, c:c + 128].reshape(512, 128).T

    for s in range(2):
        for p in range(3):
            b0, b1, b2 = bits[p], bits[(p + 1) % 3], bits[(p + 2) % 3]
            rs_copies[p, s].wait_recv()
            base = 4 * b0 if s == 0 else 4 * b0 + 2 * b1
            land = 0 if s == 0 else 4
            half = 2 if s == 0 else 1
            turn = b1 if s == 0 else b2
            out = pl.ds(base + half * (1 - turn), half)
            got = pl.ds(land + half * (1 - turn), half)
            rsb[p][out] = (rsb[p][out].astype(F32) + rbb[p][got].astype(F32)).astype(BF)
            rs_start(p, s + 1)
        a_copies[s + 1].wait_recv()
        a_send[s + 3] = a_send[s + 2] + a_got[s + 1]
        a_copies.append(remote(a_send.at[s + 3], a_got.at[s + 2], a_s.at[s + 2], a_r.at[s + 2], near[s + 1]))
        a_copies[s + 2].start()
        for p in range(3):
            b0, b1, b2 = bits[p], bits[(p + 1) % 3], bits[(p + 2) % 3]
            base = 4 * b0 if s == 0 else 4 * b0 + 2 * b1
            land = 0 if s == 0 else 4
            half = 2 if s == 0 else 1
            turn = b1 if s == 0 else b2
            keep = pl.ds(base + half * turn, half)
            got = pl.ds(land + half * turn, half)
            rsb[p][keep] = (rsb[p][keep].astype(F32) + rbb[p][got].astype(F32)).astype(BF)
    a_copies[3].wait_recv()
    a_sum = a_send[4] + a_got[3]
    unit_head = a_sum[0:1, :]
    cots = a_sum[4:8, 0:128]
    lanes = lax.broadcasted_iota(jnp.int32, (ROWS, 128), 1)
    subs = lax.broadcasted_iota(jnp.int32, (ROWS, 128), 0)
    serve = jnp.zeros((ROWS, 128), F32)
    train = jnp.zeros((ROWS, 128), F32)
    train_k = 32 * (subs // 4) + 4 * j + subs % 4
    for r in range(4):
        row = jnp.broadcast_to(cots[r:r + 1], (ROWS, 128))
        serve = serve + jnp.where(order_tile[r:r + 1, :] == subs + block * ROWS, row, 0.0)
        train = train + jnp.where(lanes + 128 * r == train_k, row, 0.0)
    cot_serve = jnp.sum(serve, axis=1, keepdims=True)
    cot_train = jnp.sum(train, axis=1, keepdims=True)

    for p in range(3):
        b0, b1, b2 = bits[p], bits[(p + 1) % 3], bits[(p + 2) % 3]
        rs_copies[p, 2].wait_recv()
        here = pl.ds(4 * b0 + 2 * b1 + b2, 1)
        sums[:, CUTS[p]:CUTS[p + 1]] = (rsb[p][here].astype(F32) + rbb[p][6:7].astype(F32))[0]

    gate, up = sums[:, 0:HALF], sums[:, HALF:2 * HALF]
    sig = jax.nn.sigmoid(gate)
    swish = gate * sig
    hidden = (swish * up).astype(BF).astype(F32)
    back = cot_serve * unit_head
    gate_low = (back * up * sig * (1.0 + gate * (1.0 - sig))).astype(BF)
    up_low = (back * swish).astype(BF)
    low = jnp.concatenate([gate_low, up_low], axis=1)

    ag_copies = {}

    def ag_start(p, s):
        b0, b1, b2 = bits[p], bits[(p + 1) % 3], bits[(p + 2) % 3]
        first, count = ((4 * b0 + 2 * b1 + b2, 1), (4 * b0 + 2 * b1, 2), (4 * b0, 4))[s]
        where = lbb[p].at[pl.ds(first, count)]
        ag_copies[p, s] = remote(where, where, ag_s.at[3 * p + s], ag_r.at[3 * p + s], near[(p + 2 - s) % 3])
        ag_copies[p, s].start()

    for p in range(3):
        b0, b1, b2 = bits[p], bits[(p + 1) % 3], bits[(p + 2) % 3]
        lbb[p][pl.ds(4 * b0 + 2 * b1 + b2, 1)] = low[:, CUTS[p]:CUTS[p + 1]][None]
        ag_start(p, 0)

    b_send[...] = jnp.zeros_like(b_send)
    b_send[0, 0:1, :] = jnp.sum(hidden * cot_serve, axis=0, keepdims=True)
    score_col = jnp.sum(hidden * unit_head, axis=1, keepdims=True)
    score_row = jnp.sum(jnp.where(lanes == subs, score_col, 0.0), axis=0, keepdims=True)
    subs8 = lax.broadcasted_iota(jnp.int32, (8, 128), 0)
    b_send[0, 8:16, 0:128] = jnp.where(subs8 == block, score_row, 0.0)
    b_copies = [remote(b_send.at[0], b_got.at[0], b_s.at[0], b_r.at[0], near[0])]
    b_copies[0].start()

    for s in range(2):
        for p in range(3):
            ag_copies[p, s].wait_recv()
            ag_start(p, s + 1)
        b_copies[s].wait_recv()
        b_send[s + 1] = b_send[s] + b_got[s]
        b_copies.append(remote(b_send.at[s + 1], b_got.at[s + 1], b_s.at[s + 1], b_r.at[s + 1], near[s + 1]))
        b_copies[s + 1].start()
    b_copies[2].wait_recv()
    b_send[3] = b_send[2] + b_got[2]
    b_copies.append(remote(b_send.at[3], b_got.at[3], b_s.at[3], b_r.at[3], sib))
    b_copies[3].start()
    for p in range(3):
        ag_copies[p, 2].wait_recv()

    lows = [jnp.concatenate([lbb[p][slot(p, blk)] for blk in range(BLOCKS)], axis=0) for p in range(3)]

    def back_tile(v, lo):
        total = dot_t(lows[0], wb[v, lo:lo + 256, CUTS[0]:CUTS[1]])
        for p in (1, 2):
            total = total + dot_t(lows[p], wb[v, lo:lo + 256, CUTS[p]:CUTS[p + 1]])
        return total

    z_copies = []
    for n, lo in enumerate((0, 256)):
        z_send[n] = back_tile(1, lo).astype(BF)
        z_copies.append(remote(z_send.at[n], z_got.at[n], z_s.at[n], z_r.at[n], sib))
        z_copies[n].start()
    for n, lo in enumerate((0, 256)):
        total = back_tile(0, lo)
        z_copies[n].wait_recv()
        z_perm[:, lo:lo + 256] = dot(place[...], (total + z_got[n].astype(F32)).astype(BF)).astype(BF)
    t_copies = [None]
    for k in range(1, 8):
        there = xor(j, k, 3)
        rows = pl.ds(pl.multiple_of(there * ROWS, ROWS), ROWS)
        t_copies.append(remote(z_perm.at[rows], t_got.at[k - 1], t_s.at[k - 1], t_r.at[k - 1], t_peer[k]))
        t_copies[k].start()
    b_copies[3].wait_recv()
    vec_out[pl.ds(core, 1)] = b_send[3, 0:8, :][None]
    vec_out[pl.ds(1 - core, 1)] = b_got[3, 0:8, :][None]
    s_send[...] = b_send[3, 8:16, 0:128] + b_got[3, 8:16, 0:128]
    sc_copies = [None]
    for k in range(1, 8):
        sc_copies.append(remote(s_send, s_got.at[k - 1], sc_s.at[k - 1], sc_r.at[k - 1], t_peer[k]))
        sc_copies[k].start()

    for p in range(3):
        for lo, hi in col_tiles(p):
            g_sib[:, lo:hi] = dot(xt[1], lows[p][:, lo - CUTS[p]:hi - CUTS[p]]).astype(BF)
    g_copies = [
        remote(g_sib.at[:, pl.ds(0, HALF)], gate_out.at[:, mine], g_s.at[0], g_r.at[0], sib),
        remote(g_sib.at[:, pl.ds(HALF, HALF)], up_out.at[:, mine], g_s.at[1], g_r.at[1], sib),
    ]
    for copy in g_copies:
        copy.start()
    for p in range(3):
        for lo, hi in col_tiles(p):
            g_own[:, lo:hi] = dot(xt[0], lows[p][:, lo - CUTS[p]:hi - CUTS[p]]).astype(BF)
    g_local = [
        pltpu.make_async_copy(g_own.at[:, pl.ds(0, HALF)], gate_out.at[:, mine], loc.at[3]),
        pltpu.make_async_copy(g_own.at[:, pl.ds(HALF, HALF)], up_out.at[:, mine], loc.at[4]),
    ]
    for copy in g_local:
        copy.start()

    total = z_perm[pl.ds(pl.multiple_of(j * ROWS, ROWS), ROWS)].astype(F32)
    for k in range(1, 8):
        t_copies[k].wait_recv()
        total = total + t_got[k - 1].astype(F32)
    total = total + cot_train * head_in[...].astype(F32)
    low_rows = total.astype(BF)
    stacked = jnp.concatenate([low_rows[:, c:c + 128] for c in range(0, 512, 128)], axis=0)
    want = lax.broadcasted_iota(jnp.int32, (256, 256), 0)
    have = lax.broadcasted_iota(jnp.int32, (256, 256), 1)
    source = ((want // 4) % 4) * 64 + (want // 16) * 4 + want % 4
    d_send[...] = dot((have == source).astype(BF), stacked).astype(BF).reshape(16, 16, 128)
    d_copies = [None]
    for k in range(1, 16):
        there = xor(i, k, 4)
        d_copies.append(remote(d_send.at[there], d_got.at[i], d_s.at[k - 1], d_r.at[k - 1], d_peer[k]))
        d_copies[k].start()
    d_got[pl.ds(i, 1)] = d_send[pl.ds(i, 1)]

    score = s_send[...]
    for k in range(1, 8):
        sc_copies[k].wait_recv()
        score = score + s_got[k - 1]
    score = jnp.sum(jnp.where(subs8 == j, score, 0.0), axis=0, keepdims=True)
    score_out[...] = jnp.broadcast_to(score + a_sum[1:2, 0:128], (8, 128))

    for k in range(1, 16):
        d_copies[k].wait_recv()
    rows_out[...] = d_got[...]

    sent = x_copies[1:] + cot_copies[1:] + w_copies + forward + a_copies[1:] + b_copies + z_copies
    sent = sent + t_copies[1:] + sc_copies[1:] + d_copies[1:]
    sent = sent + [rs_copies[p, s] for p in range(3) for s in range(3)]
    sent = sent + [ag_copies[p, s] for p in range(3) for s in range(3)]
    for copy in sent:
        copy.wait_send()
    for copy in g_copies:
        copy.wait()
    for copy in g_local:
        copy.wait()


def per_device(inputs, ordering, cotangent, gate_weight, up_weight, down_weight, value_head):
    i = lax.axis_index("dp")
    j = lax.axis_index("tensor")
    order_col = ordering.reshape(16, 8, 4).transpose(1, 0, 2).reshape(512, 1)
    order_tile = jnp.pad(ordering.reshape(4, 128), ((0, 4), (0, 0)))
    spot = jnp.arange(512, dtype=jnp.int32) - (32 * i + 4 * j)
    cot = sum(jnp.where(spot == r, cotangent[r], 0.0) for r in range(4))
    cot_tile = jnp.pad(cot.reshape(4, 128), ((0, 4), (0, 0)))
    whole = pl.BlockSpec(memory_space=pl.ANY)
    held = pl.BlockSpec(memory_space=pltpu.VMEM)
    dma = pltpu.SemaphoreType.DMA
    widths = [CUTS[p + 1] - CUTS[p] for p in range(3)]
    gate_grad, up_grad, vec, score, rows = pl.pallas_call(
        kernel,
        name="critic",
        out_shape=(
            jax.ShapeDtypeStruct((512, 1792), BF),
            jax.ShapeDtypeStruct((512, 1792), BF),
            jax.ShapeDtypeStruct((2, 8, HALF), F32),
            jax.ShapeDtypeStruct((8, 128), F32),
            jax.ShapeDtypeStruct((16, 16, 128), BF),
        ),
        in_specs=[held] * 5 + [whole] * 3,
        out_specs=(whole, whole, held, held, held),
        scratch_shapes=[
            pltpu.VMEM((2, 8, ROWS, 512), BF),
            pltpu.VMEM((2, 512, 512), BF),
            pltpu.VMEM((2, 512, 2 * HALF), BF),
            pltpu.VMEM((2 * HALF, 512), BF),
            pltpu.VMEM((512, 512), BF),
            *[pltpu.VMEM((8, ROWS, w), BF) for w in widths],
            *[pltpu.VMEM((7, ROWS, w), BF) for w in widths],
            *[pltpu.VMEM((8, ROWS, w), BF) for w in widths],
            pltpu.VMEM((7, 8, 128), F32),
            pltpu.VMEM((5, 8, HALF), F32),
            pltpu.VMEM((4, 8, HALF), F32),
            pltpu.VMEM((ROWS, 2 * HALF), F32),
            pltpu.VMEM((4, 16, HALF), F32),
            pltpu.VMEM((4, 16, HALF), F32),
            pltpu.VMEM((2, 512, 256), BF),
            pltpu.VMEM((2, 512, 256), BF),
            pltpu.VMEM((512, 512), BF),
            pltpu.VMEM((7, ROWS, 512), BF),
            pltpu.VMEM((8, 128), F32),
            pltpu.VMEM((7, 8, 128), F32),
            pltpu.VMEM((512, 2 * HALF), BF),
            pltpu.VMEM((512, 2 * HALF), BF),
            pltpu.VMEM((16, 16, 128), BF),
            pltpu.VMEM((16, 16, 128), BF),
            dma((7,)), dma((7,)), dma((7,)), dma((7,)), dma((8,)), dma((8,)), dma((2,)), dma((2,)),
            dma((5,)), dma((9,)), dma((9,)), dma((4,)), dma((4,)), dma((9,)), dma((9,)), dma((4,)), dma((4,)),
            dma((2,)), dma((2,)), dma((7,)), dma((7,)), dma((7,)), dma((7,)), dma((2,)), dma((2,)),
            dma((15,)), dma((15,)),
        ],
        compiler_params=pltpu.CompilerParams(
            collective_id=0, has_side_effects=True, vmem_limit_bytes=56 * 2**20
        ),
        cost_estimate=pl.CostEstimate(flops=6 * 10**9, bytes_accessed=12 * 10**6, transcendentals=10**5),
    )(inputs, order_col, order_tile, cot_tile, value_head.reshape(1, 512), gate_weight, up_weight, down_weight)
    down_grad = (vec[:, 0, :].reshape(2 * HALF)[:, None] * value_head.astype(F32)[None, :]).astype(BF)
    input_grad = rows.reshape(16, 4, 4, 128).transpose(2, 0, 1, 3).reshape(4, 8192)
    return (score[0, :ROWS], input_grad, gate_grad, up_grad, down_grad)


def solution(mesh):
    placed = (
        P("tensor", "dp"),
        P(),
        P(("dp", "tensor")),
        P("dp", "tensor"),
        P("dp", "tensor"),
        P("tensor", "dp"),
        P("dp"),
    )
    return jax.shard_map(
        per_device,
        mesh=mesh,
        in_specs=placed,
        out_specs=(
            P("tensor"),
            P(("dp", "tensor"), None),
            P("dp", "tensor"),
            P("dp", "tensor"),
            P("tensor", "dp"),
        ),
        check_vma=False,
    )
```

```python
import functools

import jax
import jax.numpy as jnp
from jax import lax
from jax.experimental import pallas as pl
from jax.experimental.pallas import tpu as pltpu
from jax.sharding import PartitionSpec as P

BF = jnp.bfloat16
F32 = jnp.float32
MESH = pl.DeviceIdType.MESH
HALF = 896
CHUNKS = 2
ROWS = 64
PART = ROWS // CHUNKS
CUTS = ((0, 640, 1280, 2 * HALF), (0, 512, 1152, 2 * HALF), (0, 640, 1152, 2 * HALF), (0, 640, 1280, 2 * HALF))


def dot(a, b):
    return jnp.dot(a, b, preferred_element_type=F32)


def dot_t(a, b):
    return lax.dot_general(a, b, (((1,), (1,)), ((), ())), preferred_element_type=F32)


def iota(shape, dim):
    return lax.broadcasted_iota(jnp.int32, shape, dim)


def xor(value, k, width):
    out = 0
    for b in range(width):
        bit = (value // (1 << b)) % 2
        out = out + ((1 - bit) if (k >> b) & 1 else bit) * (1 << b)
    return out


def kernel(
    x_hbm, order_hbm, head_hbm, cot_hbm, gate_w, up_w, down_w,
    gate_out, up_out, down_out, score_out, rows_out,
    x_in, order_in, head_in, cot_in, xs, xp, wb, down_v, place, rs, rb, lb, cot_own, cot_got, a_send, a_got, b_send, b_got,
    z_send, z_got, z_own, t_got, s_send, s_got, g_sib, d_send,
    x_s, x_r, cot_s, cot_r, xf_s, xf_r, w_s, w_r, loc, rs_s, rs_r, a_s, a_r, ag_s, ag_r, b_s, b_r,
    z_s, z_r, t_s, t_r, sc_s, sc_r, g_s, g_r, d_s, d_r,
):
    i = lax.axis_index("dp")
    j = lax.axis_index("tensor")
    core = i % 2
    x = (i // 2) % 4
    y = i // 8
    bits = (((x + 1) // 2) % 2, x // 2, y)
    block = bits[0] + 2 * bits[1] + 4 * bits[2]
    sib = (i + 1 - 2 * core, j)
    near = (
        (y * 8 + (x + 1 - 2 * (x % 2)) * 2 + core, j),
        (y * 8 + (3 - x) * 2 + core, j),
        ((1 - y) * 8 + x * 2 + core, j),
    )
    t_peer = [None] + [(i, xor(j, k, 3)) for k in range(1, 8)]
    d_peer = [None] + [(xor(i, k, 4), j) for k in range(1, 16)]
    sent = []

    def remote(src, dst, send, recv, device):
        copy = pltpu.make_async_remote_copy(
            src_ref=src, dst_ref=dst, send_sem=send, recv_sem=recv, device_id=device, device_id_type=MESH
        )
        copy.start()
        sent.append(copy)
        return copy

    mine = pl.ds(pl.multiple_of(core * HALF, 128), HALF)
    other = pl.ds(pl.multiple_of((1 - core) * HALF, 128), HALF)
    gates, ups = pl.ds(0, HALF), pl.ds(HALF, HALF)

    barrier = pltpu.get_barrier_semaphore()
    far = (6, 5, 7, 4, 2, 1, 3)
    for device in [t_peer[k] for k in far] + d_peer[:0:-1]:
        pl.semaphore_signal(barrier, inc=1, device_id=device, device_id_type=MESH)
    local = [
        pltpu.make_async_copy(down_w, down_v, loc.at[0]),
        pltpu.make_async_copy(gate_w.at[:, mine], wb.at[0, :, gates], loc.at[1]),
        pltpu.make_async_copy(up_w.at[:, mine], wb.at[0, :, ups], loc.at[2]),
    ]
    small = [
        pltpu.make_async_copy(x_hbm, x_in, loc.at[3]),
        pltpu.make_async_copy(order_hbm, order_in, loc.at[4]),
        pltpu.make_async_copy(head_hbm, head_in, loc.at[5]),
        pltpu.make_async_copy(cot_hbm, cot_in, loc.at[6]),
    ]
    for copy in small + local:
        copy.start()
    for copy in small:
        copy.wait()
    spot = iota((8, 128), 0) * 128 + iota((8, 128), 1) - (32 * i + 4 * j)
    cot_tile = jnp.zeros((8, 128), F32)
    for r in range(4):
        cot_tile = jnp.where(spot == r, cot_in[r], cot_tile)
    cot_own[...] = cot_tile
    pl.semaphore_wait(barrier, 22)
    x_copies = {k: remote(x_in, xs.at[0, j], x_s.at[k], x_r.at[k], t_peer[k]) for k in far}
    forward = [remote(x_in, xs.at[1, j], xf_s.at[0], xf_r.at[0], sib)]
    w_copies = [
        remote(gate_w.at[:, other], wb.at[1, :, gates], w_s.at[0], w_r.at[0], sib),
        remote(up_w.at[:, other], wb.at[1, :, ups], w_s.at[1], w_r.at[1], sib),
    ]
    cot_copies = [remote(cot_own, cot_got.at[k], cot_s.at[k], cot_r.at[k], t_peer[k]) for k in far]
    xs[0, pl.ds(j, 1)] = x_in[...][None]
    head_row = head_in[...].reshape(1, 512)
    order_row = order_in[...].reshape(1, 512)
    head_rows = jnp.broadcast_to(head_row, (16, 512))
    x_head = dot_t(head_rows, x_in[...])
    local[0].wait()
    a_send[...] = jnp.zeros_like(a_send)
    a_send[0, 0:1, :] = dot_t(head_rows, down_v[mine, :])[0:1]
    a_send[1, 0:1, :] = dot_t(head_rows, down_v[other, :])[0:1]
    for v in range(2):
        a_send[v, 1:2, 0:ROWS] = x_head[0:1]
    n = iota((512, 512), 0)
    hot = (n == jnp.broadcast_to(order_row, (512, 512))).astype(BF)
    turn = iota((512, 512), 1) == 32 * ((n // 4) % 16) + 4 * (n // 64) + n % 4
    place[...] = dot_t(turn.astype(BF), hot).astype(BF)
    for k in (1, 3, 2, 4, 5, 7, 6):
        x_copies[k].wait_recv()
        there = xor(j, k, 3)
        forward.append(remote(xs.at[0, there], xs.at[1, there], xf_s.at[k], xf_r.at[k], sib))
    def permute(v):
        for c in (0, 256):
            xp[v, :, c:c + 256] = dot(place[...], xs[v, :, :, c:c + 256].reshape(512, 256)).astype(BF)

    permute(0)
    for copy in local[1:]:
        copy.wait()
    for copy in forward + w_copies:
        copy.wait_recv()
    permute(1)
    def view(h, p, fixed, flip=None):
        where = [pl.ds(0, 2)] * 3
        for d in fixed:
            where[2 - d] = pl.ds(bits[d], 1)
        if flip is not None:
            where[2 - flip] = pl.ds(1 - bits[flip], 1)
        return (h, *where, slice(None), pl.ds(CUTS[h][p], CUTS[h][p + 1] - CUTS[h][p]))

    def dims(p):
        return [p, (p + 1) % 3, (p + 2) % 3]

    rs_copies, ag_copies = {}, {}

    def rs_start(h, p, s):
        order = dims(p)
        part = view(h, p, order[:s], order[s])
        k = 9 * h + 3 * p + s
        rs_copies[h, p, s] = remote(rs.at[part], rb.at[(s, *part)], rs_s.at[k], rs_r.at[k], near[order[s]])

    def ag_start(h, p, s):
        order = dims(p)
        part = view(h, p, order[:3 - s])
        k = 9 * h + 3 * p + s
        ag_copies[h, p, s] = remote(lb.at[part], lb.at[part], ag_s.at[k], ag_r.at[k], near[order[2 - s]])

    def x_part(v, h):
        rows = [xp[v, b * ROWS + h * PART:b * ROWS + (h + 1) * PART, :] for b in range(8)]
        return jnp.concatenate(rows, axis=0)

    for h in range(CHUNKS):
        x_own, x_sib = x_part(0, h), x_part(1, h)
        done = 0
        for lo in range(0, 2 * HALF, 256):
            cols = slice(lo, lo + 256)
            part = dot(x_own, wb[0, :, cols]) + dot(x_sib, wb[1, :, cols])
            rs[h, :, :, :, :, cols] = part.astype(BF).reshape(2, 2, 2, PART, 256)
            while done < 3 and lo + 256 >= CUTS[h][done + 1]:
                rs_start(h, done, 0)
                done += 1
        if h == 0:
            for copy in cot_copies:
                copy.wait_recv()
            for k in range(1, 8):
                cot_tile = cot_tile + cot_got[k]
            for v in range(2):
                a_send[v, 4:8, 0:128] = cot_tile[0:4]
            a_copies = [remote(a_send.at[1], a_got.at[0], a_s.at[0], a_r.at[0], sib)]
        if h == 1:
            a_copies[0].wait_recv()
            a_send[2] = a_send[0] + a_got[0]
            a_copies.append(remote(a_send.at[2], a_got.at[1], a_s.at[1], a_r.at[1], near[0]))

    def rs_add(h, p, s, own):
        order = dims(p)
        if own:
            part = view(h, p, order[:s + 2])
        else:
            part = view(h, p, order[:s + 1], order[s + 1])
        rs[part] = (rs[part].astype(F32) + rb[(s, *part)].astype(F32)).astype(BF)

    for s in range(2):
        for h in range(CHUNKS):
            for p in range(3):
                rs_copies[h, p, s].wait_recv()
                rs_add(h, p, s, False)
                rs_start(h, p, s + 1)
            for p in range(3):
                rs_add(h, p, s, True)
        a_copies[s + 1].wait_recv()
        a_send[s + 3] = a_send[s + 2] + a_got[s + 1]
        a_copies.append(remote(a_send.at[s + 3], a_got.at[s + 2], a_s.at[s + 2], a_r.at[s + 2], near[s + 1]))
    a_copies[3].wait_recv()
    a_sum = a_send[4] + a_got[3]
    unit_head = a_sum[0:1, :]
    cots = a_sum[4:8, 0:128]
    lanes, subs = iota((PART, 128), 1), iota((PART, 128), 0)

    def cot_rows(owner, h):
        train_k = 32 * ((subs + h * PART) // 4) + 4 * owner + subs % 4
        total = jnp.zeros((PART, 128), F32)
        for r in range(4):
            row = jnp.broadcast_to(cots[r:r + 1], (PART, 128))
            total = total + jnp.where(lanes + 128 * r == train_k, row, 0.0)
        return jnp.sum(total, axis=1, keepdims=True)

    sub8 = iota((8, 128), 0)
    vec = jnp.zeros((1, HALF), F32)
    score = jnp.zeros((1, 128), F32)
    for h in range(CHUNKS):
        cot_here = cot_rows(block, h)
        back = cot_here * unit_head
        summed = []
        for p in range(3):
            rs_copies[h, p, 2].wait_recv()
            part = view(h, p, (0, 1, 2))
            width = CUTS[h][p + 1] - CUTS[h][p]
            summed.append((rs[part].astype(F32) + rb[(2, *part)].astype(F32)).reshape(PART, width))
        summed = jnp.concatenate(summed, axis=1)
        gate, up = summed[:, 0:HALF], summed[:, HALF:2 * HALF]
        sig = jax.nn.sigmoid(gate)
        swish = gate * sig
        gate_low = (back * up * sig * (1.0 + gate * (1.0 - sig))).astype(BF)
        up_low = (back * swish).astype(BF)
        spot = (h, pl.ds(bits[2], 1), pl.ds(bits[1], 1), pl.ds(bits[0], 1), slice(None))
        lb[(*spot, gates)] = gate_low.reshape(1, 1, 1, PART, HALF)
        lb[(*spot, ups)] = up_low.reshape(1, 1, 1, PART, HALF)
        for p in range(3):
            ag_start(h, p, 0)
        hidden = (swish * up).astype(BF).astype(F32)
        vec = vec + jnp.sum(hidden * cot_here, axis=0, keepdims=True)
        score_col = jnp.sum(hidden * unit_head, axis=1, keepdims=True)
        spot = lanes == subs + h * PART + ROWS * (block % 2)
        score = score + jnp.sum(jnp.where(spot, score_col, 0.0), axis=0, keepdims=True)

    b_send[...] = jnp.zeros_like(b_send)
    b_send[0, 0:1, :] = vec
    b_send[0, 8:16, 0:128] = jnp.where(sub8 == block // 2, score, 0.0)
    b_copies = [remote(b_send.at[0], b_got.at[0], b_s.at[0], b_r.at[0], near[0])]
    for s in range(2):
        for h in range(CHUNKS):
            for p in range(3):
                ag_copies[h, p, s].wait_recv()
                ag_start(h, p, s + 1)
        b_copies[s].wait_recv()
        b_send[s + 1] = b_send[s] + b_got[s]
        b_copies.append(remote(b_send.at[s + 1], b_got.at[s + 1], b_s.at[s + 1], b_r.at[s + 1], near[s + 1]))
    def low(h):
        return lb[h].reshape(8 * PART, 2 * HALF)

    z_copies, t_copies = [], {}
    for h in range(CHUNKS):
        for p in range(3):
            ag_copies[h, p, 2].wait_recv()
        for c in (0, 256):
            z_send[h, :, c:c + 256] = dot_t(low(h), wb[1, c:c + 256, :]).astype(BF)
        z_copies.append(remote(z_send.at[h], z_got.at[h], z_s.at[h], z_r.at[h], sib))
        own = [dot_t(low(h), wb[0, c:c + 256, :]) for c in (0, 256)]
        z_copies[h].wait_recv()
        for n, c in enumerate((0, 256)):
            both = own[n] + z_got[h, :, c:c + 256].astype(F32)
            z_own[h, :, :, c:c + 256] = both.astype(BF).reshape(8, PART, 256)
        for k in far:
            t_copies[h, k] = remote(
                z_own.at[h, xor(j, k, 3)], t_got.at[h, k], t_s.at[8 * h + k], t_r.at[8 * h + k], t_peer[k]
            )
        if h == 0:
            b_copies[2].wait_recv()
            b_send[3] = b_send[2] + b_got[2]
            b_copies.append(remote(b_send.at[3], b_got.at[3], b_s.at[3], b_r.at[3], sib))
    b_copies[3].wait_recv()
    s_send[...] = b_send[3, 8:16, 0:128] + b_got[3, 8:16, 0:128]
    sc_copies = [remote(s_send, s_got.at[k], sc_s.at[k], sc_r.at[k], t_peer[k]) for k in range(1, 8)]
    def grad(v, lo, width):
        total = jnp.zeros((512, width), F32)
        for h in range(CHUNKS):
            lows = lb[h, :, :, :, :, lo:lo + width].reshape(8 * PART, width)
            total = total + lax.dot_general(
                x_part(v, h), lows, (((0,), (0,)), ((), ())), preferred_element_type=F32
            )
        return total.astype(BF)

    for lo in range(0, 2 * HALF, 256):
        g_sib[:, lo:lo + 256] = grad(1, lo, 256)
    g_copies = [
        remote(g_sib.at[:, gates], gate_out.at[:, mine], g_s.at[0], g_r.at[0], sib),
        remote(g_sib.at[:, ups], up_out.at[:, mine], g_s.at[1], g_r.at[1], sib),
    ]
    for first, out in ((0, gate_out), (HALF, up_out)):
        for lo, width in ((0, 256), (256, 256), (512, 256), (768, 128)):
            where = pl.ds(pl.multiple_of(core * HALF + lo, 128), width)
            out[:, where] = grad(0, first + lo, width)

    want, have = iota((4 * PART, 4 * PART), 0), iota((4 * PART, 4 * PART), 1)
    source = ((want // 4) % 4) * PART + (want // 16) * 4 + want % 4
    gather = (have == source).astype(BF)
    each = 16 // CHUNKS
    seat = i % each

    def d_copy(h, k):
        there = each * h + xor(seat, k, 3)
        return pltpu.make_async_remote_copy(
            src_ref=d_send.at[there], dst_ref=rows_out.at[i],
            send_sem=d_s.at[each * h + k], recv_sem=d_r.at[each * (i // each) + k],
            device_id=(there, j), device_id_type=MESH,
        )

    for h in range(CHUNKS):
        total = z_own[h, pl.ds(j, 1)].reshape(PART, 512).astype(F32)
        for k in far:
            t_copies[h, k].wait_recv()
            total = total + t_got[h, k].astype(F32)
        low_rows = (total + cot_rows(j, h) * head_row.astype(F32)).astype(BF)
        stacked = jnp.concatenate([low_rows[:, c:c + 128] for c in range(0, 512, 128)], axis=0)
        d_send[each * h:each * (h + 1)] = dot(gather, stacked).astype(BF).reshape(each, 16, 128)
        for k in range(each - 1, -1, -1):
            if k:
                d_copy(h, k).start()
            else:
                pl.when(i // each != h)(d_copy(h, 0).start)
    rows_out[pl.ds(i, 1)] = d_send[pl.ds(i, 1)]

    score = s_send[...]
    for k in range(1, 8):
        sc_copies[k - 1].wait_recv()
        score = score + s_got[k]
    score = jnp.concatenate([score[r:r + 1] for r in range(4)], axis=1)
    high = score.astype(BF)
    rest = score - high.astype(F32)
    middle = rest.astype(BF)
    last = (rest - middle.astype(F32)).astype(BF)
    split = jnp.concatenate([high, middle, last, jnp.zeros((13, 512), BF)], axis=0)
    moved = dot(split, place[...])
    moved = moved[0:1] + moved[1:2] + moved[2:3]
    score = a_sum[1:2, 0:ROWS]
    for b in range(8):
        score = score + jnp.where(j == b, moved[:, b * ROWS:(b + 1) * ROWS], 0.0)
    score_out[...] = jnp.zeros_like(score_out)
    score_out[0:1, 0:ROWS] = score
    head_float = head_row.astype(F32)
    for v, source in ((core, b_send), (1 - core, b_got)):
        for c in range(0, HALF, 128):
            column = jnp.broadcast_to(source[3, 0:1, c:c + 128], (128, 128)).T
            rows = pl.ds(pl.multiple_of(v * HALF + c, 128), 128)
            down_out[rows, :] = (jnp.concatenate([column] * 4, axis=1) * head_float).astype(BF)
    for half in range(CHUNKS):
        for k in range(each):
            got = pltpu.make_async_remote_copy(
                src_ref=d_send.at[0], dst_ref=rows_out.at[each * half + xor(seat, k, 3)],
                send_sem=d_s.at[0], recv_sem=d_r.at[each * half + k],
                device_id=sib, device_id_type=MESH,
            )
            if k:
                got.wait_recv()
                d_copy(half, k).wait_send()
            else:
                pl.when(i // each != half)(got.wait_recv)
                pl.when(i // each != half)(d_copy(half, 0).wait_send)
    for copy in g_copies:
        copy.wait_recv()
    for copy in sent:
        copy.wait_send()


def finish_kernel(gate_in, up_in, down_in, score_in, rows_in, gate_out, up_out, down_out, score_out, rows_out, sem):
    copies = [
        pltpu.make_async_copy(gate_in, gate_out, sem.at[0]),
        pltpu.make_async_copy(up_in, up_out, sem.at[1]),
        pltpu.make_async_copy(down_in, down_out, sem.at[2]),
    ]
    for copy in copies:
        copy.start()
    score_out[...] = score_in[0:1, 0:ROWS].reshape(ROWS)
    rows = rows_in[...].astype(F32).reshape(256, 128)
    rows_out[...] = jnp.concatenate([rows[4 * n:4 * n + 4] for n in range(64)], axis=1).astype(BF)
    for copy in copies:
        copy.wait()


def per_device(inputs, ordering, cotangent, gate_weight, up_weight, down_weight, value_head):
    whole = pl.BlockSpec(memory_space=pl.ANY)
    held = pl.BlockSpec(memory_space=pltpu.VMEM)
    dma = pltpu.SemaphoreType.DMA
    cube = (CHUNKS, 2, 2, 2, PART, 2 * HALF)
    gate_grad, up_grad, down_grad, score, rows = pl.pallas_call(
        kernel,
        name="critic",
        out_shape=(
            pltpu.VMEM((512, 2 * HALF), BF),
            pltpu.VMEM((512, 2 * HALF), BF),
            pltpu.VMEM((2 * HALF, 512), BF),
            pltpu.VMEM((8, 128), F32),
            pltpu.VMEM((16, 16, 128), BF),
        ),
        in_specs=[whole] * 7,
        out_specs=(held,) * 5,
        scratch_shapes=[
            pltpu.VMEM((ROWS, 512), BF),
            pltpu.VMEM((512,), jnp.int32),
            pltpu.VMEM((512,), BF),
            pltpu.SMEM((4,), F32),
            pltpu.VMEM((2, 8, ROWS, 512), BF),
            pltpu.VMEM((2, 512, 512), BF),
            pltpu.VMEM((2, 512, 2 * HALF), BF),
            pltpu.VMEM((2 * HALF, 512), BF),
            pltpu.VMEM((512, 512), BF),
            pltpu.VMEM(cube, BF),
            pltpu.VMEM((3, *cube), BF),
            pltpu.VMEM(cube, BF),
            pltpu.VMEM((8, 128), F32),
            pltpu.VMEM((8, 8, 128), F32),
            pltpu.VMEM((5, 8, HALF), F32),
            pltpu.VMEM((4, 8, HALF), F32),
            pltpu.VMEM((4, 16, HALF), F32),
            pltpu.VMEM((4, 16, HALF), F32),
            pltpu.VMEM((CHUNKS, 8 * PART, 512), BF),
            pltpu.VMEM((CHUNKS, 8 * PART, 512), BF),
            pltpu.VMEM((CHUNKS, 8, PART, 512), BF),
            pltpu.VMEM((CHUNKS, 8, PART, 512), BF),
            pltpu.VMEM((8, 128), F32),
            pltpu.VMEM((8, 8, 128), F32),
            pltpu.VMEM((512, 2 * HALF), BF),
            pltpu.VMEM((16, 16, 128), BF),
            *[dma((8,))] * 6, dma((2,)), dma((2,)), dma((7,)), dma((9 * CHUNKS,)), dma((9 * CHUNKS,)),
            dma((4,)), dma((4,)), dma((9 * CHUNKS,)), dma((9 * CHUNKS,)), dma((4,)), dma((4,)),
            dma((CHUNKS,)), dma((CHUNKS,)), dma((8 * CHUNKS,)), dma((8 * CHUNKS,)), dma((8,)), dma((8,)), dma((2,)), dma((2,)), dma((16,)), dma((16,)),
        ],
        compiler_params=pltpu.CompilerParams(
            collective_id=0, has_side_effects=True, vmem_limit_bytes=44 * 2**20
        ),
        cost_estimate=pl.CostEstimate(flops=6 * 10**9, bytes_accessed=12 * 10**6, transcendentals=10**5),
    )(*[
        pltpu.with_memory_space_constraint(a, pltpu.HBM)
        for a in (inputs, ordering, value_head, cotangent, gate_weight, up_weight, down_weight)
    ])
    score, rows, gate_grad, up_grad, down_grad = finish_call(gate_grad, up_grad, down_grad, score, rows)
    return (score, rows, gate_grad, up_grad, down_grad)


def finish_call(gate_grad, up_grad, down_grad, score, rows):
    whole = pl.BlockSpec(memory_space=pl.ANY)
    held = pl.BlockSpec(memory_space=pltpu.VMEM)
    outs = pl.pallas_call(
        finish_kernel,
        name="deliver",
        out_shape=(
            jax.ShapeDtypeStruct((512, 2 * HALF), BF),
            jax.ShapeDtypeStruct((512, 2 * HALF), BF),
            jax.ShapeDtypeStruct((2 * HALF, 512), BF),
            jax.ShapeDtypeStruct((ROWS,), F32),
            jax.ShapeDtypeStruct((4, 8192), BF),
        ),
        in_specs=[whole] * 3 + [held] * 2,
        out_specs=(whole,) * 3 + (held,) * 2,
        scratch_shapes=[pltpu.SemaphoreType.DMA((3,))],
        compiler_params=pltpu.CompilerParams(vmem_limit_bytes=8 * 2**20),
    )(gate_grad, up_grad, down_grad, score, rows)
    return outs[3], outs[4], outs[0], outs[1], outs[2]


def solution(mesh):
    placed = (
        P("tensor", "dp"),
        P(),
        P(("dp", "tensor")),
        P("dp", "tensor"),
        P("dp", "tensor"),
        P("tensor", "dp"),
        P("dp"),
    )
    return jax.shard_map(
        per_device,
        mesh=mesh,
        in_specs=placed,
        out_specs=(
            P("tensor"),
            P(("dp", "tensor"), None),
            P("dp", "tensor"),
            P("dp", "tensor"),
            P("tensor", "dp"),
        ),
        check_vma=False,
    )
```

```python
import functools

import jax
import jax.numpy as jnp
from jax import lax
from jax.experimental import pallas as pl
from jax.experimental.pallas import tpu as pltpu
from jax.sharding import PartitionSpec as P

BF = jnp.bfloat16
F32 = jnp.float32
MESH = pl.DeviceIdType.MESH
HALF = 896
CHUNKS = 2
ROWS = 64
PART = ROWS // CHUNKS
CHUNKS = 2
STEP, SHIFT = 3.0, 1.1
ROWS = 64
PART = ROWS // CHUNKS
CUTS = ((0, 640, 1280, 2 * HALF), (0, 512, 1152, 2 * HALF), (0, 640, 1152, 2 * HALF), (0, 640, 1280, 2 * HALF))


def dot(a, b):
    return jnp.dot(a, b, preferred_element_type=F32)


def dot_t(a, b):
    return lax.dot_general(a, b, (((1,), (1,)), ((), ())), preferred_element_type=F32)


def iota(shape, dim):
    return lax.broadcasted_iota(jnp.int32, shape, dim)


def xor(value, k, width):
    out = 0
    for b in range(width):
        bit = (value // (1 << b)) % 2
        out = out + ((1 - bit) if (k >> b) & 1 else bit) * (1 << b)
    return out


def kernel(
    x_hbm, order_hbm, head_hbm, cot_hbm, gate_w, up_w, down_w,
    gate_out, up_out, down_out, score_out, rows_out,
    x_in, order_in, head_in, cot_in, xs, xp, wb, down_v, place, rs, rb, lb, cot_own, cot_got, a_send, a_got, b_send, b_got,
    z_send, z_got, z_own, t_got, s_send, s_got, g_sib, d_send,
    x_s, x_r, cot_s, cot_r, xf_s, xf_r, w_s, w_r, loc, rs_s, rs_r, a_s, a_r, ag_s, ag_r, b_s, b_r,
    z_s, z_r, t_s, t_r, sc_s, sc_r, g_s, g_r, d_s, d_r,
):
    i = lax.axis_index("dp")
    j = lax.axis_index("tensor")
    core = i % 2
    x = (i // 2) % 4
    y = i // 8
    bits = (((x + 1) // 2) % 2, x // 2, y)
    block = bits[0] + 2 * bits[1] + 4 * bits[2]
    sib = (i + 1 - 2 * core, j)

    def flip(*turned):
        at = x
        if 0 in turned:
            at = at + 1 - 2 * (at % 2)
        if 1 in turned:
            at = 3 - at
        return (((1 - y) if 2 in turned else y) * 8 + at * 2 + core, j)

    near = (flip(0), flip(1), flip(2))
    chips = [flip(0, 1, 2), flip(0, 1), flip(0, 2), flip(1, 2), flip(2), flip(1), flip(0)]

    def fold(row):
        return jnp.concatenate([row[:, c:c + 128] for c in range(0, HALF, 128)], axis=0)

    def unfold(tile):
        return jnp.concatenate([tile[r:r + 1] for r in range(HALF // 128)], axis=1)

    t_peer = [None] + [(i, xor(j, k, 3)) for k in range(1, 8)]
    d_peer = [None] + [(xor(i, k, 4), j) for k in range(1, 16)]
    sent = []

    def remote(src, dst, send, recv, device):
        copy = pltpu.make_async_remote_copy(
            src_ref=src, dst_ref=dst, send_sem=send, recv_sem=recv, device_id=device, device_id_type=MESH
        )
        copy.start()
        sent.append(copy)
        return copy

    mine = pl.ds(pl.multiple_of(core * HALF, 128), HALF)
    other = pl.ds(pl.multiple_of((1 - core) * HALF, 128), HALF)
    gates, ups = pl.ds(0, HALF), pl.ds(HALF, HALF)

    barrier = pltpu.get_barrier_semaphore()
    far = (6, 5, 7, 4, 2, 1, 3)
    for device in [t_peer[k] for k in far] + d_peer[:0:-1]:
        pl.semaphore_signal(barrier, inc=1, device_id=device, device_id_type=MESH)
    local = [
        pltpu.make_async_copy(down_w, down_v, loc.at[0]),
        pltpu.make_async_copy(gate_w.at[:, mine], wb.at[0, :, gates], loc.at[1]),
        pltpu.make_async_copy(up_w.at[:, mine], wb.at[0, :, ups], loc.at[2]),
    ]
    small = [
        pltpu.make_async_copy(x_hbm, x_in, loc.at[3]),
        pltpu.make_async_copy(order_hbm, order_in, loc.at[4]),
        pltpu.make_async_copy(head_hbm, head_in, loc.at[5]),
        pltpu.make_async_copy(cot_hbm, cot_in, loc.at[6]),
    ]
    for copy in small + local:
        copy.start()
    for copy in small:
        copy.wait()
    spot = iota((8, 128), 0) * 128 + iota((8, 128), 1) - (32 * i + 4 * j)
    cot_tile = jnp.zeros((8, 128), F32)
    for r in range(4):
        cot_tile = jnp.where(spot == r, cot_in[r], cot_tile)
    cot_own[...] = cot_tile
    pl.semaphore_wait(barrier, 22)
    cot_copies = [remote(cot_own, cot_got.at[k], cot_s.at[k], cot_r.at[k], t_peer[k]) for k in far]
    x_copies = {k: remote(x_in, xs.at[0, j], x_s.at[k], x_r.at[k], t_peer[k]) for k in far}
    forward = [remote(x_in, xs.at[1, j], xf_s.at[0], xf_r.at[0], sib)]
    w_copies = [
        remote(gate_w.at[:, other], wb.at[1, :, gates], w_s.at[0], w_r.at[0], sib),
        remote(up_w.at[:, other], wb.at[1, :, ups], w_s.at[1], w_r.at[1], sib),
    ]
    xs[0, pl.ds(j, 1)] = x_in[...][None]
    head_row = head_in[...].reshape(1, 512)
    order_row = order_in[...].reshape(1, 512)
    head_rows = jnp.broadcast_to(head_row, (16, 512))
    x_head = dot_t(head_rows, x_in[...])
    local[0].wait()
    a_send[...] = jnp.zeros_like(a_send)
    a_send[0, 0:7, :] = fold(dot_t(head_rows, down_v[mine, :])[0:1])
    a_send[1, 0:7, :] = fold(dot_t(head_rows, down_v[other, :])[0:1])
    for v in range(2):
        a_send[v, 7:8, 0:ROWS] = x_head[0:1]
    n = iota((512, 512), 0)
    hot = (n == jnp.broadcast_to(order_row, (512, 512))).astype(BF)
    turn = iota((512, 512), 1) == 32 * ((n // 4) % 16) + 4 * (n // 64) + n % 4
    place[...] = dot_t(turn.astype(BF), hot).astype(BF)
    a_copies, b_copies = [], []

    def a_first():
        for copy in cot_copies:
            copy.wait_recv()
        total = cot_tile
        for k in range(1, 8):
            total = total + cot_got[k]
        for v in range(2):
            a_send[v, 8:12, :] = total[0:4]
        a_copies.append(remote(a_send.at[1], a_got.at[7], a_s.at[7], a_r.at[7], sib))

    def a_second():
        a_copies[0].wait_recv()
        a_send[2] = a_send[0] + a_got[7]
        for n, device in enumerate(chips):
            a_copies.append(remote(a_send.at[2], a_got.at[n], a_s.at[n], a_r.at[n], device))

    def a_last():
        total = a_send[2]
        for n in range(7):
            a_copies[n + 1].wait_recv()
            total = total + a_got[n]
        return total

    def b_first(vec, score):
        b_send[0, 0:7, :] = fold(vec)
        b_send[0, 7:8, :] = jnp.zeros((1, 128), F32)
        b_send[0, 8:16, :] = jnp.where(sub8 == block // 2, score, 0.0)
        for n, device in enumerate(chips):
            b_copies.append(remote(b_send.at[0], b_got.at[n], b_s.at[n], b_r.at[n], device))

    def b_second():
        total = b_send[0]
        for n in range(7):
            b_copies[n].wait_recv()
            total = total + b_got[n]
        b_send[1] = total
        b_copies.append(remote(b_send.at[1], b_got.at[7], b_s.at[7], b_r.at[7], sib))

    for k in (1, 3, 2, 4, 5, 7, 6):
        x_copies[k].wait_recv()
        there = xor(j, k, 3)
        forward.append(remote(xs.at[0, there], xs.at[1, there], xf_s.at[k], xf_r.at[k], sib))

    def permute(v):
        for c in (0, 256):
            xp[v, :, c:c + 256] = dot(place[...], xs[v, :, :, c:c + 256].reshape(512, 256)).astype(BF)

    permute(0)
    a_first()
    for copy in local[1:]:
        copy.wait()
    for copy in forward + w_copies:
        copy.wait_recv()
    permute(1)
    a_second()
    def view(h, p, fixed, turned=()):
        where = [pl.ds(0, 2)] * 3
        for d in fixed:
            where[2 - d] = pl.ds(1 - bits[d] if d in turned else bits[d], 1)
        return (h, *where, slice(None), pl.ds(CUTS[h][p], CUTS[h][p + 1] - CUTS[h][p]))

    def turns(p):
        b, c = (p + 1) % 3, (p + 2) % 3
        return ((b, c), (b,), (c,))

    every = (0, 1, 2)
    rs_copies, ag_copies = {}, {}

    def rs_first(h, p):
        part = view(h, p, (p,), (p,))
        k = 12 * h + 4 * p
        rs_copies[h, p, 0] = remote(rs.at[part], rb.at[(0, *part)], rs_s.at[k], rs_r.at[k], near[p])

    def rs_second(h, p):
        for n, turned in enumerate(turns(p)):
            part = view(h, p, every, turned)
            k = 12 * h + 4 * p + n + 1
            rs_copies[h, p, n + 1] = remote(
                rs.at[part], rb.at[(n + 1, *part)], rs_s.at[k], rs_r.at[k], flip(*turned)
            )

    def ag_first(h, p):
        part = view(h, p, every)
        for n, turned in enumerate(turns(p)):
            k = 12 * h + 4 * p + n + 1
            ag_copies[h, p, n + 1] = remote(lb.at[part], lb.at[part], ag_s.at[k], ag_r.at[k], flip(*turned))

    def ag_second(h, p):
        part = view(h, p, (p,))
        k = 12 * h + 4 * p
        ag_copies[h, p, 0] = remote(lb.at[part], lb.at[part], ag_s.at[k], ag_r.at[k], near[p])

    def x_part(v, h):
        rows = [xp[v, b * ROWS + h * PART:b * ROWS + (h + 1) * PART, :] for b in range(8)]
        return jnp.concatenate(rows, axis=0)

    def products(h):
        x_own, x_sib = x_part(0, h), x_part(1, h)
        done = 0
        for lo in range(0, 2 * HALF, 256):
            cols = slice(lo, lo + 256)
            part = dot(x_own, wb[0, :, cols]) + dot(x_sib, wb[1, :, cols])
            rs[h, :, :, :, :, cols] = part.astype(BF).reshape(2, 2, 2, PART, 256)
            while done < 3 and lo + 256 >= CUTS[h][done + 1]:
                rs_first(h, done)
                done += 1

    def halve(h):
        for p in range(3):
            rs_copies[h, p, 0].wait_recv()
            part = view(h, p, (p,))
            rs[part] = (rs[part].astype(F32) + rb[(0, *part)].astype(F32)).astype(BF)
            rs_second(h, p)

    lanes, subs = iota((PART, 128), 1), iota((PART, 128), 0)
    sub8 = iota((8, 128), 0)
    state = {}

    def cot_rows(owner, h):
        train_k = 32 * ((subs + h * PART) // 4) + 4 * owner + subs % 4
        total = jnp.zeros((PART, 128), F32)
        for r in range(4):
            row = jnp.broadcast_to(state["cots"][r:r + 1], (PART, 128))
            total = total + jnp.where(lanes + 128 * r == train_k, row, 0.0)
        return jnp.sum(total, axis=1, keepdims=True)

    def middle(h):
        if h == 0:
            state["sum"] = a_last()
            state["cots"] = state["sum"][8:12]
            state["head"] = unfold(state["sum"])
            state["vec"] = jnp.zeros((1, HALF), F32)
            state["score"] = jnp.zeros((1, 128), F32)
        unit_head = state["head"]
        cot_here = cot_rows(block, h)
        back = cot_here * unit_head
        summed = []
        for p in range(3):
            part = view(h, p, every)
            total = rs[part].astype(F32)
            for n in (2, 3, 1):
                rs_copies[h, p, n].wait_recv()
                total = total + rb[(n, *part)].astype(F32)
            summed.append(total.reshape(PART, CUTS[h][p + 1] - CUTS[h][p]))
        summed = jnp.concatenate(summed, axis=1)
        gate, up = summed[:, 0:HALF], summed[:, HALF:2 * HALF]
        sig = jax.nn.sigmoid(gate)
        swish = gate * sig
        gate_low = (back * up * sig * (1.0 + gate * (1.0 - sig))).astype(BF)
        up_low = (back * swish).astype(BF)
        spot = (h, pl.ds(bits[2], 1), pl.ds(bits[1], 1), pl.ds(bits[0], 1), slice(None))
        lb[(*spot, gates)] = gate_low.reshape(1, 1, 1, PART, HALF)
        lb[(*spot, ups)] = up_low.reshape(1, 1, 1, PART, HALF)
        for p in range(3):
            ag_first(h, p)
        hidden = (swish * up).astype(BF).astype(F32)
        state["vec"] = state["vec"] + jnp.sum(hidden * cot_here, axis=0, keepdims=True)
        score_col = jnp.sum(hidden * unit_head, axis=1, keepdims=True)
        spot = lanes == subs + h * PART + ROWS * (block % 2)
        state["score"] = state["score"] + jnp.sum(jnp.where(spot, score_col, 0.0), axis=0, keepdims=True)
        if h == CHUNKS - 1:
            b_first(state["vec"], state["score"])

    def spread(h):
        for p in range(3):
            for n in (2, 3, 1):
                ag_copies[h, p, n].wait_recv()
            ag_second(h, p)

    def low(h):
        return lb[h].reshape(8 * PART, 2 * HALF)

    def back_products(h):
        for p in range(3):
            ag_copies[h, p, 0].wait_recv()
        for c in (0, 256):
            z_send[h, :, c:c + 256] = dot_t(low(h), wb[1, c:c + 256, :]).astype(BF)
        z_copies[h] = remote(z_send.at[h], z_got.at[h], z_s.at[h], z_r.at[h], sib)
        own = [dot_t(low(h), wb[0, c:c + 256, :]) for c in (0, 256)]
        z_copies[h].wait_recv()
        for n, c in enumerate((0, 256)):
            both = own[n] + z_got[h, :, c:c + 256].astype(F32)
            z_own[h, :, :, c:c + 256] = both.astype(BF).reshape(8, PART, 256)
        for k in far:
            t_copies[h, k] = remote(
                z_own.at[h, xor(j, k, 3)], t_got.at[h, k], t_s.at[8 * h + k], t_r.at[8 * h + k], t_peer[k]
            )

    z_copies, t_copies = {}, {}
    events = sorted((h * SHIFT + e * STEP, h, e) for h in range(CHUNKS) for e in range(5))
    for _, h, e in events:
        (products, halve, middle, spread, back_products)[e](h)
        if h == CHUNKS - 1 and e == 3:
            b_second()
    b_copies[7].wait_recv()
    s_send[...] = b_send[1, 8:16] + b_got[7, 8:16]
    sc_copies = [remote(s_send, s_got.at[k], sc_s.at[k], sc_r.at[k], t_peer[k]) for k in range(1, 8)]
    def grad(v, lo, width):
        lows = [lb[h, :, :, :, :, lo:lo + width].reshape(8 * PART, width) for h in range(CHUNKS)]
        rows = [x_part(v, h) for h in range(CHUNKS)]
        return lax.dot_general(
            jnp.concatenate(rows, axis=0), jnp.concatenate(lows, axis=0), (((0,), (0,)), ((), ())),
            preferred_element_type=F32,
        ).astype(BF)

    for lo in range(0, 2 * HALF, 256):
        g_sib[:, lo:lo + 256] = grad(1, lo, 256)
    g_copies = [
        remote(g_sib.at[:, gates], gate_out.at[:, mine], g_s.at[0], g_r.at[0], sib),
        remote(g_sib.at[:, ups], up_out.at[:, mine], g_s.at[1], g_r.at[1], sib),
    ]
    for first, out in ((0, gate_out), (HALF, up_out)):
        for lo, width in ((0, 256), (256, 256), (512, 256), (768, 128)):
            where = pl.ds(pl.multiple_of(core * HALF + lo, 128), width)
            out[:, where] = grad(0, first + lo, width)

    want, have = iota((4 * PART, 4 * PART), 0), iota((4 * PART, 4 * PART), 1)
    source = ((want // 4) % 4) * PART + (want // 16) * 4 + want % 4
    gather = (have == source).astype(BF)
    each = 16 // CHUNKS
    seat = i % each

    def d_copy(h, k):
        there = each * h + xor(seat, k, each.bit_length() - 1)
        return pltpu.make_async_remote_copy(
            src_ref=d_send.at[there], dst_ref=rows_out.at[i],
            send_sem=d_s.at[each * h + k], recv_sem=d_r.at[each * (i // each) + k],
            device_id=(there, j), device_id_type=MESH,
        )

    for h in range(CHUNKS):
        total = z_own[h, pl.ds(j, 1)].reshape(PART, 512).astype(F32)
        for k in far:
            t_copies[h, k].wait_recv()
            total = total + t_got[h, k].astype(F32)
        low_rows = (total + cot_rows(j, h) * head_row.astype(F32)).astype(BF)
        stacked = jnp.concatenate([low_rows[:, c:c + 128] for c in range(0, 512, 128)], axis=0)
        d_send[each * h:each * (h + 1)] = dot(gather, stacked).astype(BF).reshape(each, 16, 128)
        for k in range(each - 1, -1, -1):
            if k:
                d_copy(h, k).start()
            else:
                pl.when(i // each != h)(d_copy(h, 0).start)
    rows_out[pl.ds(i, 1)] = d_send[pl.ds(i, 1)]

    score = s_send[...]
    for k in range(1, 8):
        sc_copies[k - 1].wait_recv()
        score = score + s_got[k]
    score = jnp.concatenate([score[r:r + 1] for r in range(4)], axis=1)
    high = score.astype(BF)
    rest = score - high.astype(F32)
    middle = rest.astype(BF)
    last = (rest - middle.astype(F32)).astype(BF)
    split = jnp.concatenate([high, middle, last, jnp.zeros((13, 512), BF)], axis=0)
    moved = dot(split, place[...])
    moved = moved[0:1] + moved[1:2] + moved[2:3]
    score = state["sum"][7:8, 0:ROWS]
    for b in range(8):
        score = score + jnp.where(j == b, moved[:, b * ROWS:(b + 1) * ROWS], 0.0)
    score_out[...] = jnp.zeros_like(score_out)
    score_out[0:1, 0:ROWS] = score
    head_float = head_row.astype(F32)
    for v, tile in ((core, b_send[1]), (1 - core, b_got[7])):
        for c in range(0, HALF, 128):
            column = jnp.broadcast_to(tile[c // 128:c // 128 + 1], (128, 128)).T
            rows = pl.ds(pl.multiple_of(v * HALF + c, 128), 128)
            down_out[rows, :] = (jnp.concatenate([column] * 4, axis=1) * head_float).astype(BF)
    for half in range(CHUNKS):
        for k in range(each):
            got = pltpu.make_async_remote_copy(
                src_ref=d_send.at[0], dst_ref=rows_out.at[each * half + xor(seat, k, each.bit_length() - 1)],
                send_sem=d_s.at[0], recv_sem=d_r.at[each * half + k],
                device_id=sib, device_id_type=MESH,
            )
            if k:
                got.wait_recv()
                d_copy(half, k).wait_send()
            else:
                pl.when(i // each != half)(got.wait_recv)
                pl.when(i // each != half)(d_copy(half, 0).wait_send)
    for copy in g_copies:
        copy.wait_recv()
    for copy in sent:
        copy.wait_send()


def finish_kernel(gate_in, up_in, down_in, score_in, rows_in, gate_out, up_out, down_out, score_out, rows_out, sem):
    copies = [
        pltpu.make_async_copy(gate_in, gate_out, sem.at[0]),
        pltpu.make_async_copy(up_in, up_out, sem.at[1]),
        pltpu.make_async_copy(down_in, down_out, sem.at[2]),
    ]
    for copy in copies:
        copy.start()
    score_out[...] = score_in[0:1, 0:ROWS].reshape(ROWS)
    rows = rows_in[...].astype(F32).reshape(256, 128)
    rows_out[...] = jnp.concatenate([rows[4 * n:4 * n + 4] for n in range(64)], axis=1).astype(BF)
    for copy in copies:
        copy.wait()


def per_device(inputs, ordering, cotangent, gate_weight, up_weight, down_weight, value_head):
    whole = pl.BlockSpec(memory_space=pl.ANY)
    held = pl.BlockSpec(memory_space=pltpu.VMEM)
    dma = pltpu.SemaphoreType.DMA
    cube = (CHUNKS, 2, 2, 2, PART, 2 * HALF)
    gate_grad, up_grad, down_grad, score, rows = pl.pallas_call(
        kernel,
        name="critic",
        out_shape=(
            pltpu.VMEM((512, 2 * HALF), BF),
            pltpu.VMEM((512, 2 * HALF), BF),
            pltpu.VMEM((2 * HALF, 512), BF),
            pltpu.VMEM((8, 128), F32),
            pltpu.VMEM((16, 16, 128), BF),
        ),
        in_specs=[whole] * 7,
        out_specs=(held,) * 5,
        scratch_shapes=[
            pltpu.VMEM((ROWS, 512), BF),
            pltpu.VMEM((512,), jnp.int32),
            pltpu.VMEM((512,), BF),
            pltpu.SMEM((4,), F32),
            pltpu.VMEM((2, 8, ROWS, 512), BF),
            pltpu.VMEM((2, 512, 512), BF),
            pltpu.VMEM((2, 512, 2 * HALF), BF),
            pltpu.VMEM((2 * HALF, 512), BF),
            pltpu.VMEM((512, 512), BF),
            pltpu.VMEM(cube, BF),
            pltpu.VMEM((4, *cube), BF),
            pltpu.VMEM(cube, BF),
            pltpu.VMEM((8, 128), F32),
            pltpu.VMEM((8, 8, 128), F32),
            pltpu.VMEM((3, 16, 128), F32),
            pltpu.VMEM((8, 16, 128), F32),
            pltpu.VMEM((2, 16, 128), F32),
            pltpu.VMEM((8, 16, 128), F32),
            pltpu.VMEM((CHUNKS, 8 * PART, 512), BF),
            pltpu.VMEM((CHUNKS, 8 * PART, 512), BF),
            pltpu.VMEM((CHUNKS, 8, PART, 512), BF),
            pltpu.VMEM((CHUNKS, 8, PART, 512), BF),
            pltpu.VMEM((8, 128), F32),
            pltpu.VMEM((8, 8, 128), F32),
            pltpu.VMEM((512, 2 * HALF), BF),
            pltpu.VMEM((16, 16, 128), BF),
            *[dma((8,))] * 6, dma((2,)), dma((2,)), dma((7,)), dma((12 * CHUNKS,)), dma((12 * CHUNKS,)),
            dma((8,)), dma((8,)), dma((12 * CHUNKS,)), dma((12 * CHUNKS,)), dma((8,)), dma((8,)),
            dma((CHUNKS,)), dma((CHUNKS,)), dma((8 * CHUNKS,)), dma((8 * CHUNKS,)), dma((8,)), dma((8,)), dma((2,)), dma((2,)), dma((16,)), dma((16,)),
        ],
        compiler_params=pltpu.CompilerParams(
            collective_id=0, has_side_effects=True, vmem_limit_bytes=44 * 2**20
        ),
        cost_estimate=pl.CostEstimate(flops=6 * 10**9, bytes_accessed=12 * 10**6, transcendentals=10**5),
    )(*[
        pltpu.with_memory_space_constraint(a, pltpu.HBM)
        for a in (inputs, ordering, value_head, cotangent, gate_weight, up_weight, down_weight)
    ])
    score, rows, gate_grad, up_grad, down_grad = finish_call(gate_grad, up_grad, down_grad, score, rows)
    return (score, rows, gate_grad, up_grad, down_grad)


def finish_call(gate_grad, up_grad, down_grad, score, rows):
    whole = pl.BlockSpec(memory_space=pl.ANY)
    held = pl.BlockSpec(memory_space=pltpu.VMEM)
    outs = pl.pallas_call(
        finish_kernel,
        name="deliver",
        out_shape=(
            jax.ShapeDtypeStruct((512, 2 * HALF), BF),
            jax.ShapeDtypeStruct((512, 2 * HALF), BF),
            jax.ShapeDtypeStruct((2 * HALF, 512), BF),
            jax.ShapeDtypeStruct((ROWS,), F32),
            jax.ShapeDtypeStruct((4, 8192), BF),
        ),
        in_specs=[whole] * 3 + [held] * 2,
        out_specs=(whole,) * 3 + (held,) * 2,
        scratch_shapes=[pltpu.SemaphoreType.DMA((3,))],
        compiler_params=pltpu.CompilerParams(vmem_limit_bytes=8 * 2**20),
    )(gate_grad, up_grad, down_grad, score, rows)
    return outs[3], outs[4], outs[0], outs[1], outs[2]


def solution(mesh):
    placed = (
        P("tensor", "dp"),
        P(),
        P(("dp", "tensor")),
        P("dp", "tensor"),
        P("dp", "tensor"),
        P("tensor", "dp"),
        P("dp"),
    )
    return jax.shard_map(
        per_device,
        mesh=mesh,
        in_specs=placed,
        out_specs=(
            P("tensor"),
            P(("dp", "tensor"), None),
            P("dp", "tensor"),
            P("dp", "tensor"),
            P("tensor", "dp"),
        ),
        check_vma=False,
    )
```

```python
import functools

import jax
import jax.numpy as jnp
from jax import lax
from jax.experimental import pallas as pl
from jax.experimental.pallas import tpu as pltpu
from jax.sharding import PartitionSpec as P

BF = jnp.bfloat16
F32 = jnp.float32
MESH = pl.DeviceIdType.MESH
HALF = 896
CHUNKS = 4
STEP = 3.0
STARTS = (0.0, 0.3, 1.6, 2.6)
GROUPS = ((0, 2), (2, 1), (3, 1))
ROWS = 64
PART = ROWS // CHUNKS
CUTS = ((0, 640, 1280, 2 * HALF), (0, 512, 1152, 2 * HALF), (0, 640, 1152, 2 * HALF), (0, 640, 1280, 2 * HALF))


def dot(a, b):
    return jnp.dot(a, b, preferred_element_type=F32)


def dot_t(a, b):
    return lax.dot_general(a, b, (((1,), (1,)), ((), ())), preferred_element_type=F32)


def iota(shape, dim):
    return lax.broadcasted_iota(jnp.int32, shape, dim)


def xor(value, k, width):
    out = 0
    for b in range(width):
        bit = (value // (1 << b)) % 2
        out = out + ((1 - bit) if (k >> b) & 1 else bit) * (1 << b)
    return out


def kernel(
    x_hbm, order_hbm, head_hbm, cot_hbm, gate_w, up_w, down_w,
    gate_out, up_out, down_out, score_out, rows_out,
    x_in, order_in, head_in, cot_in, xs, xp, wb, down_v, place, rs, rb, lb, cot_own, cot_got, a_send, a_got, b_send, b_got,
    z_send, z_got, z_own, t_got, s_send, s_got, g_sib, d_send,
    x_s, x_r, cot_s, cot_r, xf_s, xf_r, w_s, w_r, loc, rs_s, rs_r, a_s, a_r, ag_s, ag_r, b_s, b_r,
    z_s, z_r, t_s, t_r, sc_s, sc_r, g_s, g_r, d_s, d_r,
):
    i = lax.axis_index("dp")
    j = lax.axis_index("tensor")
    core = i % 2
    x = (i // 2) % 4
    y = i // 8
    bits = (((x + 1) // 2) % 2, x // 2, y)
    block = bits[0] + 2 * bits[1] + 4 * bits[2]
    sib = (i + 1 - 2 * core, j)

    def flip(*turned):
        at = x
        if 0 in turned:
            at = at + 1 - 2 * (at % 2)
        if 1 in turned:
            at = 3 - at
        return (((1 - y) if 2 in turned else y) * 8 + at * 2 + core, j)

    near = (flip(0), flip(1), flip(2))
    chips = [flip(0, 1, 2), flip(0, 1), flip(0, 2), flip(1, 2), flip(2), flip(1), flip(0)]

    def fold(row):
        return jnp.concatenate([row[:, c:c + 128] for c in range(0, HALF, 128)], axis=0)

    def unfold(tile):
        return jnp.concatenate([tile[r:r + 1] for r in range(HALF // 128)], axis=1)

    t_peer = [None] + [(i, xor(j, k, 3)) for k in range(1, 8)]
    d_peer = [None] + [(xor(i, k, 4), j) for k in range(1, 16)]
    sent = []

    def remote(src, dst, send, recv, device):
        copy = pltpu.make_async_remote_copy(
            src_ref=src, dst_ref=dst, send_sem=send, recv_sem=recv, device_id=device, device_id_type=MESH
        )
        copy.start()
        sent.append(copy)
        return copy

    mine = pl.ds(pl.multiple_of(core * HALF, 128), HALF)
    other = pl.ds(pl.multiple_of((1 - core) * HALF, 128), HALF)
    gates, ups = pl.ds(0, HALF), pl.ds(HALF, HALF)

    barrier = pltpu.get_barrier_semaphore()
    far = (6, 5, 7, 4, 2, 1, 3)
    for device in [t_peer[k] for k in far] + d_peer[:0:-1]:
        pl.semaphore_signal(barrier, inc=1, device_id=device, device_id_type=MESH)
    local = [
        pltpu.make_async_copy(down_w, down_v, loc.at[0]),
        pltpu.make_async_copy(gate_w.at[:, mine], wb.at[0, :, gates], loc.at[1]),
        pltpu.make_async_copy(up_w.at[:, mine], wb.at[0, :, ups], loc.at[2]),
    ]
    small = [
        pltpu.make_async_copy(x_hbm, x_in, loc.at[3]),
        pltpu.make_async_copy(order_hbm, order_in, loc.at[4]),
        pltpu.make_async_copy(head_hbm, head_in, loc.at[5]),
        pltpu.make_async_copy(cot_hbm, cot_in, loc.at[6]),
    ]
    for copy in small + local:
        copy.start()
    for copy in small:
        copy.wait()
    spot = iota((8, 128), 0) * 128 + iota((8, 128), 1) - (32 * i + 4 * j)
    cot_tile = jnp.zeros((8, 128), F32)
    for r in range(4):
        cot_tile = jnp.where(spot == r, cot_in[r], cot_tile)
    cot_own[...] = cot_tile
    pl.semaphore_wait(barrier, 22)
    cot_copies = [remote(cot_own, cot_got.at[k], cot_s.at[k], cot_r.at[k], t_peer[k]) for k in far]
    x_copies = {k: remote(x_in, xs.at[0, j], x_s.at[k], x_r.at[k], t_peer[k]) for k in far}
    forward = [remote(x_in, xs.at[1, j], xf_s.at[0], xf_r.at[0], sib)]
    w_copies = [
        remote(gate_w.at[:, other], wb.at[1, :, gates], w_s.at[0], w_r.at[0], sib),
        remote(up_w.at[:, other], wb.at[1, :, ups], w_s.at[1], w_r.at[1], sib),
    ]
    xs[0, pl.ds(j, 1)] = x_in[...][None]
    head_row = head_in[...].reshape(1, 512)
    order_row = order_in[...].reshape(1, 512)
    head_rows = jnp.broadcast_to(head_row, (16, 512))
    x_head = dot_t(head_rows, x_in[...])
    local[0].wait()
    a_send[...] = jnp.zeros_like(a_send)
    a_send[0, 0:7, :] = fold(dot_t(head_rows, down_v[mine, :])[0:1])
    a_send[1, 0:7, :] = fold(dot_t(head_rows, down_v[other, :])[0:1])
    for v in range(2):
        a_send[v, 7:8, 0:ROWS] = x_head[0:1]
    n = iota((512, 512), 0)
    hot = (n == jnp.broadcast_to(order_row, (512, 512))).astype(BF)
    turn = iota((512, 512), 1) == 32 * ((n // 4) % 16) + 4 * (n // 64) + n % 4
    place[...] = dot_t(turn.astype(BF), hot).astype(BF)
    a_copies, b_copies = [], []

    def a_first():
        for copy in cot_copies:
            copy.wait_recv()
        total = cot_tile
        for k in range(1, 8):
            total = total + cot_got[k]
        for v in range(2):
            a_send[v, 8:12, :] = total[0:4]
        a_copies.append(remote(a_send.at[1], a_got.at[7], a_s.at[7], a_r.at[7], sib))

    def a_second():
        a_copies[0].wait_recv()
        a_send[2] = a_send[0] + a_got[7]
        for n, device in enumerate(chips):
            a_copies.append(remote(a_send.at[2], a_got.at[n], a_s.at[n], a_r.at[n], device))

    def a_last():
        total = a_send[2]
        for n in range(7):
            a_copies[n + 1].wait_recv()
            total = total + a_got[n]
        return total

    def b_first(vec, score):
        b_send[0, 0:7, :] = fold(vec)
        b_send[0, 7:8, :] = jnp.zeros((1, 128), F32)
        b_send[0, 8:16, :] = jnp.where(sub8 == block // 2, score, 0.0)
        for n, device in enumerate(chips):
            b_copies.append(remote(b_send.at[0], b_got.at[n], b_s.at[n], b_r.at[n], device))

    def b_second():
        total = b_send[0]
        for n in range(7):
            b_copies[n].wait_recv()
            total = total + b_got[n]
        b_send[1] = total
        b_copies.append(remote(b_send.at[1], b_got.at[7], b_s.at[7], b_r.at[7], sib))

    for k in (1, 3, 2, 4, 5, 7, 6):
        x_copies[k].wait_recv()
        there = xor(j, k, 3)
        forward.append(remote(xs.at[0, there], xs.at[1, there], xf_s.at[k], xf_r.at[k], sib))

    def permute(v):
        for c in (0, 256):
            xp[v, :, c:c + 256] = dot(place[...], xs[v, :, :, c:c + 256].reshape(512, 256)).astype(BF)

    permute(0)
    a_first()
    for copy in local[1:]:
        copy.wait()
    for copy in forward + w_copies:
        copy.wait_recv()
    permute(1)
    a_second()
    def view(h, p, fixed, turned=()):
        where = [pl.ds(0, 2)] * 3
        for d in fixed:
            where[2 - d] = pl.ds(1 - bits[d] if d in turned else bits[d], 1)
        return (h, *where, slice(None), pl.ds(CUTS[h][p], CUTS[h][p + 1] - CUTS[h][p]))

    def turns(p):
        b, c = (p + 1) % 3, (p + 2) % 3
        return ((b, c), (b,), (c,))

    every = (0, 1, 2)
    rs_copies, ag_copies = {}, {}

    def rs_first(h, p):
        part = view(h, p, (p,), (p,))
        k = 12 * h + 4 * p
        rs_copies[h, p, 0] = remote(rs.at[part], rb.at[(0, *part)], rs_s.at[k], rs_r.at[k], near[p])

    def rs_second(h, p):
        for n, turned in enumerate(turns(p)):
            part = view(h, p, every, turned)
            k = 12 * h + 4 * p + n + 1
            rs_copies[h, p, n + 1] = remote(
                rs.at[part], rb.at[(n + 1, *part)], rs_s.at[k], rs_r.at[k], flip(*turned)
            )

    def ag_first(h, p):
        part = view(h, p, every)
        for n, turned in enumerate(turns(p)):
            k = 12 * h + 4 * p + n + 1
            ag_copies[h, p, n + 1] = remote(lb.at[part], lb.at[part], ag_s.at[k], ag_r.at[k], flip(*turned))

    def ag_second(h, p):
        part = view(h, p, (p,))
        k = 12 * h + 4 * p
        ag_copies[h, p, 0] = remote(lb.at[part], lb.at[part], ag_s.at[k], ag_r.at[k], near[p])

    def x_part(v, h):
        rows = [xp[v, b * ROWS + h * PART:b * ROWS + (h + 1) * PART, :] for b in range(8)]
        return jnp.concatenate(rows, axis=0)

    def products(h):
        x_own, x_sib = x_part(0, h), x_part(1, h)
        done = 0
        for lo in range(0, 2 * HALF, 256):
            cols = slice(lo, lo + 256)
            part = dot(x_own, wb[0, :, cols]) + dot(x_sib, wb[1, :, cols])
            rs[h, :, :, :, :, cols] = part.astype(BF).reshape(2, 2, 2, PART, 256)
            while done < 3 and lo + 256 >= CUTS[h][done + 1]:
                rs_first(h, done)
                done += 1

    def halve(h):
        for p in range(3):
            rs_copies[h, p, 0].wait_recv()
            part = view(h, p, (p,))
            rs[part] = (rs[part].astype(F32) + rb[(0, *part)].astype(F32)).astype(BF)
            rs_second(h, p)

    lanes, subs = iota((PART, 128), 1), iota((PART, 128), 0)
    sub8 = iota((8, 128), 0)
    state = {}

    def cot_rows(owner, h):
        train_k = 32 * ((subs + h * PART) // 4) + 4 * owner + subs % 4
        total = jnp.zeros((PART, 128), F32)
        for r in range(4):
            row = jnp.broadcast_to(state["cots"][r:r + 1], (PART, 128))
            total = total + jnp.where(lanes + 128 * r == train_k, row, 0.0)
        return jnp.sum(total, axis=1, keepdims=True)

    def middle(h):
        if h == 0:
            state["sum"] = a_last()
            state["cots"] = state["sum"][8:12]
            state["head"] = unfold(state["sum"])
            state["vec"] = jnp.zeros((1, HALF), F32)
            state["score"] = jnp.zeros((1, 128), F32)
        unit_head = state["head"]
        cot_here = cot_rows(block, h)
        back = cot_here * unit_head
        summed = []
        for p in range(3):
            part = view(h, p, every)
            total = rs[part].astype(F32)
            for n in (2, 3, 1):
                rs_copies[h, p, n].wait_recv()
                total = total + rb[(n, *part)].astype(F32)
            summed.append(total.reshape(PART, CUTS[h][p + 1] - CUTS[h][p]))
        summed = jnp.concatenate(summed, axis=1)
        gate, up = summed[:, 0:HALF], summed[:, HALF:2 * HALF]
        sig = jax.nn.sigmoid(gate)
        swish = gate * sig
        gate_low = (back * up * sig * (1.0 + gate * (1.0 - sig))).astype(BF)
        up_low = (back * swish).astype(BF)
        spot = (h, pl.ds(bits[2], 1), pl.ds(bits[1], 1), pl.ds(bits[0], 1), slice(None))
        lb[(*spot, gates)] = gate_low.reshape(1, 1, 1, PART, HALF)
        lb[(*spot, ups)] = up_low.reshape(1, 1, 1, PART, HALF)
        for p in range(3):
            ag_first(h, p)
        hidden = (swish * up).astype(BF).astype(F32)
        state["vec"] = state["vec"] + jnp.sum(hidden * cot_here, axis=0, keepdims=True)
        score_col = jnp.sum(hidden * unit_head, axis=1, keepdims=True)
        spot = lanes == subs + h * PART + ROWS * (block % 2)
        state["score"] = state["score"] + jnp.sum(jnp.where(spot, score_col, 0.0), axis=0, keepdims=True)
        if h == CHUNKS - 1:
            b_first(state["vec"], state["score"])

    def spread(h):
        for p in range(3):
            for n in (2, 3, 1):
                ag_copies[h, p, n].wait_recv()
            ag_second(h, p)

    def low(h):
        return lb[h].reshape(8 * PART, 2 * HALF)

    def back_products(h):
        first, count = [g for g in GROUPS if g[0] <= h < g[0] + g[1]][0]
        for p in range(3):
            ag_copies[h, p, 0].wait_recv()
        if h < first + count - 1:
            return
        members = range(first, first + count)
        group = pl.ds(first, count)
        lows = jnp.concatenate([low(m) for m in members], axis=0)
        for c in (0, 256):
            part = dot_t(lows, wb[1, c:c + 256, :]).astype(BF)
            z_send[first:first + count, :, c:c + 256] = part.reshape(count, 8 * PART, 256)
        copy = remote(z_send.at[group], z_got.at[group], z_s.at[first], z_r.at[first], sib)
        own = [dot_t(lows, wb[0, c:c + 256, :]) for c in (0, 256)]
        copy.wait_recv()
        for n, c in enumerate((0, 256)):
            both = own[n].reshape(count, 8 * PART, 256) + z_got[first:first + count, :, c:c + 256].astype(F32)
            z_own[first:first + count, :, :, c:c + 256] = both.astype(BF).reshape(count, 8, PART, 256)
        for k in far:
            t_copies[first, k] = remote(
                z_own.at[group, xor(j, k, 3)], t_got.at[group, k],
                t_s.at[8 * first + k], t_r.at[8 * first + k], t_peer[k],
            )

    t_copies = {}
    events = sorted((STARTS[h] + e * STEP, h, e) for h in range(CHUNKS) for e in range(5))
    for _, h, e in events:
        (products, halve, middle, spread, back_products)[e](h)
        if h == CHUNKS - 1 and e == 3:
            b_second()
    b_copies[7].wait_recv()
    s_send[...] = b_send[1, 8:16] + b_got[7, 8:16]
    sc_copies = [remote(s_send, s_got.at[k], sc_s.at[k], sc_r.at[k], t_peer[k]) for k in range(1, 8)]
    def grad(v, lo, width):
        lows = [lb[h, :, :, :, :, lo:lo + width].reshape(8 * PART, width) for h in range(CHUNKS)]
        rows = [x_part(v, h) for h in range(CHUNKS)]
        return lax.dot_general(
            jnp.concatenate(rows, axis=0), jnp.concatenate(lows, axis=0), (((0,), (0,)), ((), ())),
            preferred_element_type=F32,
        ).astype(BF)

    for lo in range(0, 2 * HALF, 256):
        g_sib[:, lo:lo + 256] = grad(1, lo, 256)
    g_copies = [
        remote(g_sib.at[:, gates], gate_out.at[:, mine], g_s.at[0], g_r.at[0], sib),
        remote(g_sib.at[:, ups], up_out.at[:, mine], g_s.at[1], g_r.at[1], sib),
    ]
    for first, out in ((0, gate_out), (HALF, up_out)):
        for lo, width in ((0, 256), (256, 256), (512, 256), (768, 128)):
            where = pl.ds(pl.multiple_of(core * HALF + lo, 128), width)
            out[:, where] = grad(0, first + lo, width)

    want, have = iota((4 * PART, 4 * PART), 0), iota((4 * PART, 4 * PART), 1)
    source = ((want // 4) % 4) * PART + (want // 16) * 4 + want % 4
    gather = (have == source).astype(BF)
    each = 16 // CHUNKS
    seat = i % each

    def d_copy(h, k):
        there = each * h + xor(seat, k, each.bit_length() - 1)
        return pltpu.make_async_remote_copy(
            src_ref=d_send.at[there], dst_ref=rows_out.at[i],
            send_sem=d_s.at[each * h + k], recv_sem=d_r.at[each * (i // each) + k],
            device_id=(there, j), device_id_type=MESH,
        )

    for h in range(CHUNKS):
        total = z_own[h, pl.ds(j, 1)].reshape(PART, 512).astype(F32)
        for k in far:
            if (h, k) in t_copies:
                t_copies[h, k].wait_recv()
            total = total + t_got[h, k].astype(F32)
        low_rows = (total + cot_rows(j, h) * head_row.astype(F32)).astype(BF)
        stacked = jnp.concatenate([low_rows[:, c:c + 128] for c in range(0, 512, 128)], axis=0)
        d_send[each * h:each * (h + 1)] = dot(gather, stacked).astype(BF).reshape(each, 16, 128)
        for k in range(each - 1, -1, -1):
            if k:
                d_copy(h, k).start()
            else:
                pl.when(i // each != h)(d_copy(h, 0).start)
    rows_out[pl.ds(i, 1)] = d_send[pl.ds(i, 1)]

    score = s_send[...]
    for k in range(1, 8):
        sc_copies[k - 1].wait_recv()
        score = score + s_got[k]
    score = jnp.concatenate([score[r:r + 1] for r in range(4)], axis=1)
    high = score.astype(BF)
    rest = score - high.astype(F32)
    middle = rest.astype(BF)
    last = (rest - middle.astype(F32)).astype(BF)
    split = jnp.concatenate([high, middle, last, jnp.zeros((13, 512), BF)], axis=0)
    moved = dot(split, place[...])
    moved = moved[0:1] + moved[1:2] + moved[2:3]
    score = state["sum"][7:8, 0:ROWS]
    for b in range(8):
        score = score + jnp.where(j == b, moved[:, b * ROWS:(b + 1) * ROWS], 0.0)
    score_out[...] = jnp.zeros_like(score_out)
    score_out[0:1, 0:ROWS] = score
    head_float = head_row.astype(F32)
    for v, tile in ((core, b_send[1]), (1 - core, b_got[7])):
        for c in range(0, HALF, 128):
            column = jnp.broadcast_to(tile[c // 128:c // 128 + 1], (128, 128)).T
            rows = pl.ds(pl.multiple_of(v * HALF + c, 128), 128)
            down_out[rows, :] = (jnp.concatenate([column] * 4, axis=1) * head_float).astype(BF)
    for half in range(CHUNKS):
        for k in range(each):
            got = pltpu.make_async_remote_copy(
                src_ref=d_send.at[0], dst_ref=rows_out.at[each * half + xor(seat, k, each.bit_length() - 1)],
                send_sem=d_s.at[0], recv_sem=d_r.at[each * half + k],
                device_id=sib, device_id_type=MESH,
            )
            if k:
                got.wait_recv()
                d_copy(half, k).wait_send()
            else:
                pl.when(i // each != half)(got.wait_recv)
                pl.when(i // each != half)(d_copy(half, 0).wait_send)
    for copy in g_copies:
        copy.wait_recv()
    for copy in sent:
        copy.wait_send()


def finish_kernel(gate_in, up_in, down_in, score_in, rows_in, gate_out, up_out, down_out, score_out, rows_out, sem):
    copies = [
        pltpu.make_async_copy(gate_in, gate_out, sem.at[0]),
        pltpu.make_async_copy(up_in, up_out, sem.at[1]),
        pltpu.make_async_copy(down_in, down_out, sem.at[2]),
    ]
    for copy in copies:
        copy.start()
    score_out[...] = score_in[0:1, 0:ROWS].reshape(ROWS)
    rows = rows_in[...].astype(F32).reshape(256, 128)
    rows_out[...] = jnp.concatenate([rows[4 * n:4 * n + 4] for n in range(64)], axis=1).astype(BF)
    for copy in copies:
        copy.wait()


def per_device(inputs, ordering, cotangent, gate_weight, up_weight, down_weight, value_head):
    whole = pl.BlockSpec(memory_space=pl.ANY)
    held = pl.BlockSpec(memory_space=pltpu.VMEM)
    dma = pltpu.SemaphoreType.DMA
    cube = (CHUNKS, 2, 2, 2, PART, 2 * HALF)
    gate_grad, up_grad, down_grad, score, rows = pl.pallas_call(
        kernel,
        name="critic",
        out_shape=(
            pltpu.VMEM((512, 2 * HALF), BF),
            pltpu.VMEM((512, 2 * HALF), BF),
            pltpu.VMEM((2 * HALF, 512), BF),
            pltpu.VMEM((8, 128), F32),
            pltpu.VMEM((16, 16, 128), BF),
        ),
        in_specs=[whole] * 7,
        out_specs=(held,) * 5,
        scratch_shapes=[
            pltpu.VMEM((ROWS, 512), BF),
            pltpu.VMEM((512,), jnp.int32),
            pltpu.VMEM((512,), BF),
            pltpu.SMEM((4,), F32),
            pltpu.VMEM((2, 8, ROWS, 512), BF),
            pltpu.VMEM((2, 512, 512), BF),
            pltpu.VMEM((2, 512, 2 * HALF), BF),
            pltpu.VMEM((2 * HALF, 512), BF),
            pltpu.VMEM((512, 512), BF),
            pltpu.VMEM(cube, BF),
            pltpu.VMEM((4, *cube), BF),
            pltpu.VMEM(cube, BF),
            pltpu.VMEM((8, 128), F32),
            pltpu.VMEM((8, 8, 128), F32),
            pltpu.VMEM((3, 16, 128), F32),
            pltpu.VMEM((8, 16, 128), F32),
            pltpu.VMEM((2, 16, 128), F32),
            pltpu.VMEM((8, 16, 128), F32),
            pltpu.VMEM((CHUNKS, 8 * PART, 512), BF),
            pltpu.VMEM((CHUNKS, 8 * PART, 512), BF),
            pltpu.VMEM((CHUNKS, 8, PART, 512), BF),
            pltpu.VMEM((CHUNKS, 8, PART, 512), BF),
            pltpu.VMEM((8, 128), F32),
            pltpu.VMEM((8, 8, 128), F32),
            pltpu.VMEM((512, 2 * HALF), BF),
            pltpu.VMEM((16, 16, 128), BF),
            *[dma((8,))] * 6, dma((2,)), dma((2,)), dma((7,)), dma((12 * CHUNKS,)), dma((12 * CHUNKS,)),
            dma((8,)), dma((8,)), dma((12 * CHUNKS,)), dma((12 * CHUNKS,)), dma((8,)), dma((8,)),
            dma((CHUNKS,)), dma((CHUNKS,)), dma((8 * CHUNKS,)), dma((8 * CHUNKS,)), dma((8,)), dma((8,)), dma((2,)), dma((2,)), dma((16,)), dma((16,)),
        ],
        compiler_params=pltpu.CompilerParams(
            collective_id=0, has_side_effects=True, vmem_limit_bytes=44 * 2**20
        ),
        cost_estimate=pl.CostEstimate(flops=6 * 10**9, bytes_accessed=12 * 10**6, transcendentals=10**5),
    )(*[
        pltpu.with_memory_space_constraint(a, pltpu.HBM)
        for a in (inputs, ordering, value_head, cotangent, gate_weight, up_weight, down_weight)
    ])
    score, rows, gate_grad, up_grad, down_grad = finish_call(gate_grad, up_grad, down_grad, score, rows)
    return (score, rows, gate_grad, up_grad, down_grad)


def finish_call(gate_grad, up_grad, down_grad, score, rows):
    whole = pl.BlockSpec(memory_space=pl.ANY)
    held = pl.BlockSpec(memory_space=pltpu.VMEM)
    outs = pl.pallas_call(
        finish_kernel,
        name="deliver",
        out_shape=(
            jax.ShapeDtypeStruct((512, 2 * HALF), BF),
            jax.ShapeDtypeStruct((512, 2 * HALF), BF),
            jax.ShapeDtypeStruct((2 * HALF, 512), BF),
            jax.ShapeDtypeStruct((ROWS,), F32),
            jax.ShapeDtypeStruct((4, 8192), BF),
        ),
        in_specs=[whole] * 3 + [held] * 2,
        out_specs=(whole,) * 3 + (held,) * 2,
        scratch_shapes=[pltpu.SemaphoreType.DMA((3,))],
        compiler_params=pltpu.CompilerParams(vmem_limit_bytes=8 * 2**20),
    )(gate_grad, up_grad, down_grad, score, rows)
    return outs[3], outs[4], outs[0], outs[1], outs[2]


def solution(mesh):
    placed = (
        P("tensor", "dp"),
        P(),
        P(("dp", "tensor")),
        P("dp", "tensor"),
        P("dp", "tensor"),
        P("tensor", "dp"),
        P("dp"),
    )
    return jax.shard_map(
        per_device,
        mesh=mesh,
        in_specs=placed,
        out_specs=(
            P("tensor"),
            P(("dp", "tensor"), None),
            P("dp", "tensor"),
            P("dp", "tensor"),
            P("tensor", "dp"),
        ),
        check_vma=False,
    )
```

```python
import functools

import jax
import jax.numpy as jnp
from jax import lax
from jax.experimental import pallas as pl
from jax.experimental.pallas import tpu as pltpu
from jax.sharding import PartitionSpec as P

BF = jnp.bfloat16
F32 = jnp.float32
MESH = pl.DeviceIdType.MESH
HALF = 896
CHUNKS = 4
STEP = 3.0
STARTS = (0.0, 0.3, 1.6, 2.6)
GROUPS = ((0, 1), (1, 1), (2, 1), (3, 1))
ROWS = 64
PART = ROWS // CHUNKS
CUTS = ((0, 640, 1280, 2 * HALF), (0, 512, 1152, 2 * HALF), (0, 640, 1152, 2 * HALF), (0, 640, 1280, 2 * HALF))


def dot(a, b):
    return jnp.dot(a, b, preferred_element_type=F32)


def dot_t(a, b):
    return lax.dot_general(a, b, (((1,), (1,)), ((), ())), preferred_element_type=F32)


def iota(shape, dim):
    return lax.broadcasted_iota(jnp.int32, shape, dim)


def xor(value, k, width):
    out = 0
    for b in range(width):
        bit = (value // (1 << b)) % 2
        out = out + ((1 - bit) if (k >> b) & 1 else bit) * (1 << b)
    return out


def kernel(
    x_hbm, order_hbm, head_hbm, cot_hbm, gate_w, up_w, down_w,
    gate_out, up_out, down_out, score_out, rows_out,
    x_in, order_in, head_in, cot_in, xs, xp, wb, down_v, place, rs, rb, lb, cot_own, cot_got, a_send, a_got, b_send, b_got,
    z_send, z_got, z_own, t_got, s_send, s_got, g_sib, d_send,
    x_s, x_r, cot_s, cot_r, xf_s, xf_r, w_s, w_r, loc, rs_s, rs_r, a_s, a_r, ag_s, ag_r, b_s, b_r,
    z_s, z_r, t_s, t_r, sc_s, sc_r, g_s, g_r, d_s, d_r,
):
    i = lax.axis_index("dp")
    j = lax.axis_index("tensor")
    core = i % 2
    x = (i // 2) % 4
    y = i // 8
    bits = (((x + 1) // 2) % 2, x // 2, y)
    block = bits[0] + 2 * bits[1] + 4 * bits[2]
    sib = (i + 1 - 2 * core, j)

    def flip(*turned):
        at = x
        if 0 in turned:
            at = at + 1 - 2 * (at % 2)
        if 1 in turned:
            at = 3 - at
        return (((1 - y) if 2 in turned else y) * 8 + at * 2 + core, j)

    near = (flip(0), flip(1), flip(2))
    chips = [flip(0, 1, 2), flip(0, 1), flip(0, 2), flip(1, 2), flip(2), flip(1), flip(0)]

    def fold(row):
        return jnp.concatenate([row[:, c:c + 128] for c in range(0, HALF, 128)], axis=0)

    def unfold(tile):
        return jnp.concatenate([tile[r:r + 1] for r in range(HALF // 128)], axis=1)

    t_peer = [None] + [(i, xor(j, k, 3)) for k in range(1, 8)]
    d_peer = [None] + [(xor(i, k, 4), j) for k in range(1, 16)]
    sent = []

    def remote(src, dst, send, recv, device):
        copy = pltpu.make_async_remote_copy(
            src_ref=src, dst_ref=dst, send_sem=send, recv_sem=recv, device_id=device, device_id_type=MESH
        )
        copy.start()
        sent.append(copy)
        return copy

    mine = pl.ds(pl.multiple_of(core * HALF, 128), HALF)
    other = pl.ds(pl.multiple_of((1 - core) * HALF, 128), HALF)
    gates, ups = pl.ds(0, HALF), pl.ds(HALF, HALF)

    barrier = pltpu.get_barrier_semaphore()
    far = (6, 5, 7, 4, 2, 1, 3)
    for device in [t_peer[k] for k in far] + d_peer[:0:-1]:
        pl.semaphore_signal(barrier, inc=1, device_id=device, device_id_type=MESH)
    local = [
        pltpu.make_async_copy(down_w, down_v, loc.at[0]),
        pltpu.make_async_copy(gate_w.at[:, mine], wb.at[0, :, gates], loc.at[1]),
        pltpu.make_async_copy(up_w.at[:, mine], wb.at[0, :, ups], loc.at[2]),
    ]
    small = [
        pltpu.make_async_copy(x_hbm, x_in, loc.at[3]),
        pltpu.make_async_copy(order_hbm, order_in, loc.at[4]),
        pltpu.make_async_copy(head_hbm, head_in, loc.at[5]),
        pltpu.make_async_copy(cot_hbm, cot_in, loc.at[6]),
    ]
    for copy in small + local:
        copy.start()
    for copy in small:
        copy.wait()
    spot = iota((8, 128), 0) * 128 + iota((8, 128), 1) - (32 * i + 4 * j)
    cot_tile = jnp.zeros((8, 128), F32)
    for r in range(4):
        cot_tile = jnp.where(spot == r, cot_in[r], cot_tile)
    cot_own[...] = cot_tile
    pl.semaphore_wait(barrier, 22)
    cot_copies = [remote(cot_own, cot_got.at[k], cot_s.at[k], cot_r.at[k], t_peer[k]) for k in far]
    x_copies = {k: remote(x_in, xs.at[0, j], x_s.at[k], x_r.at[k], t_peer[k]) for k in far}
    forward = [remote(x_in, xs.at[1, j], xf_s.at[0], xf_r.at[0], sib)]
    w_copies = [
        remote(gate_w.at[:, other], wb.at[1, :, gates], w_s.at[0], w_r.at[0], sib),
        remote(up_w.at[:, other], wb.at[1, :, ups], w_s.at[1], w_r.at[1], sib),
    ]
    xs[0, pl.ds(j, 1)] = x_in[...][None]
    head_row = head_in[...].reshape(1, 512)
    order_row = order_in[...].reshape(1, 512)
    head_rows = jnp.broadcast_to(head_row, (16, 512))
    x_head = dot_t(head_rows, x_in[...])
    local[0].wait()
    a_send[...] = jnp.zeros_like(a_send)
    a_send[0, 0:7, :] = fold(dot_t(head_rows, down_v[mine, :])[0:1])
    a_send[1, 0:7, :] = fold(dot_t(head_rows, down_v[other, :])[0:1])
    for v in range(2):
        a_send[v, 7:8, 0:ROWS] = x_head[0:1]
    n = iota((512, 512), 0)
    hot = (n == jnp.broadcast_to(order_row, (512, 512))).astype(BF)
    turn = iota((512, 512), 1) == 32 * ((n // 4) % 16) + 4 * (n // 64) + n % 4
    place[...] = dot_t(turn.astype(BF), hot).astype(BF)
    a_copies, b_copies = [], []

    def a_first():
        for copy in cot_copies:
            copy.wait_recv()
        total = cot_tile
        for k in range(1, 8):
            total = total + cot_got[k]
        for v in range(2):
            a_send[v, 8:12, :] = total[0:4]
        a_copies.append(remote(a_send.at[1], a_got.at[7], a_s.at[7], a_r.at[7], sib))

    def a_second():
        a_copies[0].wait_recv()
        a_send[2] = a_send[0] + a_got[7]
        for n, device in enumerate(chips):
            a_copies.append(remote(a_send.at[2], a_got.at[n], a_s.at[n], a_r.at[n], device))

    def a_last():
        total = a_send[2]
        for n in range(7):
            a_copies[n + 1].wait_recv()
            total = total + a_got[n]
        return total

    def b_first(vec, score):
        b_send[0, 0:7, :] = fold(vec)
        b_send[0, 7:8, :] = jnp.zeros((1, 128), F32)
        b_send[0, 8:16, :] = jnp.where(sub8 == block // 2, score, 0.0)
        for n, device in enumerate(chips):
            b_copies.append(remote(b_send.at[0], b_got.at[n], b_s.at[n], b_r.at[n], device))

    def b_second():
        total = b_send[0]
        for n in range(7):
            b_copies[n].wait_recv()
            total = total + b_got[n]
        b_send[1] = total
        b_copies.append(remote(b_send.at[1], b_got.at[7], b_s.at[7], b_r.at[7], sib))

    for k in (1, 3, 2, 4, 5, 7, 6):
        x_copies[k].wait_recv()
        there = xor(j, k, 3)
        forward.append(remote(xs.at[0, there], xs.at[1, there], xf_s.at[k], xf_r.at[k], sib))

    def permute(v):
        for c in (0, 256):
            xp[v, :, c:c + 256] = dot(place[...], xs[v, :, :, c:c + 256].reshape(512, 256)).astype(BF)

    permute(0)
    a_first()
    for copy in local[1:]:
        copy.wait()
    for copy in forward + w_copies:
        copy.wait_recv()
    permute(1)
    a_second()
    def view(h, p, fixed, turned=()):
        where = [pl.ds(0, 2)] * 3
        for d in fixed:
            where[2 - d] = pl.ds(1 - bits[d] if d in turned else bits[d], 1)
        return (h, *where, slice(None), pl.ds(CUTS[h][p], CUTS[h][p + 1] - CUTS[h][p]))

    def turns(p):
        b, c = (p + 1) % 3, (p + 2) % 3
        return ((b, c), (b,), (c,))

    every = (0, 1, 2)
    rs_copies, ag_copies = {}, {}

    def rs_first(h, p):
        part = view(h, p, (p,), (p,))
        k = 12 * h + 4 * p
        rs_copies[h, p, 0] = remote(rs.at[part], rb.at[(0, *part)], rs_s.at[k], rs_r.at[k], near[p])

    def rs_second(h, p):
        for n, turned in enumerate(turns(p)):
            part = view(h, p, every, turned)
            k = 12 * h + 4 * p + n + 1
            rs_copies[h, p, n + 1] = remote(
                rs.at[part], rb.at[(n + 1, *part)], rs_s.at[k], rs_r.at[k], flip(*turned)
            )

    def ag_first(h, p):
        part = view(h, p, every)
        for n, turned in enumerate(turns(p)):
            k = 12 * h + 4 * p + n + 1
            ag_copies[h, p, n + 1] = remote(lb.at[part], lb.at[part], ag_s.at[k], ag_r.at[k], flip(*turned))

    def ag_second(h, p):
        part = view(h, p, (p,))
        k = 12 * h + 4 * p
        ag_copies[h, p, 0] = remote(lb.at[part], lb.at[part], ag_s.at[k], ag_r.at[k], near[p])

    def x_part(v, h):
        rows = [xp[v, b * ROWS + h * PART:b * ROWS + (h + 1) * PART, :] for b in range(8)]
        return jnp.concatenate(rows, axis=0)

    def products(h):
        x_own, x_sib = x_part(0, h), x_part(1, h)
        done = 0
        for lo in range(0, 2 * HALF, 256):
            cols = slice(lo, lo + 256)
            part = dot(x_own, wb[0, :, cols]) + dot(x_sib, wb[1, :, cols])
            rs[h, :, :, :, :, cols] = part.astype(BF).reshape(2, 2, 2, PART, 256)
            while done < 3 and lo + 256 >= CUTS[h][done + 1]:
                rs_first(h, done)
                done += 1

    def halve(h):
        for p in range(3):
            rs_copies[h, p, 0].wait_recv()
            part = view(h, p, (p,))
            rs[part] = (rs[part].astype(F32) + rb[(0, *part)].astype(F32)).astype(BF)
            rs_second(h, p)

    lanes, subs = iota((PART, 128), 1), iota((PART, 128), 0)
    sub8 = iota((8, 128), 0)
    state = {}

    def cot_rows(owner, h):
        train_k = 32 * ((subs + h * PART) // 4) + 4 * owner + subs % 4
        total = jnp.zeros((PART, 128), F32)
        for r in range(4):
            row = jnp.broadcast_to(state["cots"][r:r + 1], (PART, 128))
            total = total + jnp.where(lanes + 128 * r == train_k, row, 0.0)
        return jnp.sum(total, axis=1, keepdims=True)

    def middle(h):
        if h == 0:
            state["sum"] = a_last()
            state["cots"] = state["sum"][8:12]
            state["head"] = unfold(state["sum"])
            state["vec"] = jnp.zeros((1, HALF), F32)
            state["score"] = jnp.zeros((1, 128), F32)
        unit_head = state["head"]
        cot_here = cot_rows(block, h)
        back = cot_here * unit_head
        summed = []
        for p in range(3):
            part = view(h, p, every)
            total = rs[part].astype(F32)
            for n in (2, 3, 1):
                rs_copies[h, p, n].wait_recv()
                total = total + rb[(n, *part)].astype(F32)
            summed.append(total.reshape(PART, CUTS[h][p + 1] - CUTS[h][p]))
        summed = jnp.concatenate(summed, axis=1)
        gate, up = summed[:, 0:HALF], summed[:, HALF:2 * HALF]
        sig = jax.nn.sigmoid(gate)
        swish = gate * sig
        gate_low = (back * up * sig * (1.0 + gate * (1.0 - sig))).astype(BF)
        up_low = (back * swish).astype(BF)
        spot = (h, pl.ds(bits[2], 1), pl.ds(bits[1], 1), pl.ds(bits[0], 1), slice(None))
        lb[(*spot, gates)] = gate_low.reshape(1, 1, 1, PART, HALF)
        lb[(*spot, ups)] = up_low.reshape(1, 1, 1, PART, HALF)
        for p in range(3):
            ag_first(h, p)
        hidden = (swish * up).astype(BF).astype(F32)
        state["vec"] = state["vec"] + jnp.sum(hidden * cot_here, axis=0, keepdims=True)
        score_col = jnp.sum(hidden * unit_head, axis=1, keepdims=True)
        spot = lanes == subs + h * PART + ROWS * (block % 2)
        state["score"] = state["score"] + jnp.sum(jnp.where(spot, score_col, 0.0), axis=0, keepdims=True)
        if h == CHUNKS - 1:
            b_first(state["vec"], state["score"])

    def spread(h):
        for p in range(3):
            for n in (2, 3, 1):
                ag_copies[h, p, n].wait_recv()
            ag_second(h, p)

    def low(h):
        return lb[h].reshape(8 * PART, 2 * HALF)

    def back_products(h):
        first, count = [g for g in GROUPS if g[0] <= h < g[0] + g[1]][0]
        for p in range(3):
            ag_copies[h, p, 0].wait_recv()
        if h < first + count - 1:
            return
        members = range(first, first + count)
        group = pl.ds(first, count)
        lows = jnp.concatenate([low(m) for m in members], axis=0)
        for c in (0, 256):
            part = dot_t(lows, wb[1, c:c + 256, :]).astype(BF)
            z_send[first:first + count, :, c:c + 256] = part.reshape(count, 8 * PART, 256)
        copy = remote(z_send.at[group], z_got.at[group], z_s.at[first], z_r.at[first], sib)
        own = [dot_t(lows, wb[0, c:c + 256, :]) for c in (0, 256)]
        copy.wait_recv()
        for n, c in enumerate((0, 256)):
            both = own[n].reshape(count, 8 * PART, 256) + z_got[first:first + count, :, c:c + 256].astype(F32)
            z_own[first:first + count, :, :, c:c + 256] = both.astype(BF).reshape(count, 8, PART, 256)
        for k in far:
            t_copies[first, k] = remote(
                z_own.at[group, xor(j, k, 3)], t_got.at[group, k],
                t_s.at[8 * first + k], t_r.at[8 * first + k], t_peer[k],
            )

    t_copies = {}
    events = sorted((STARTS[h] + e * STEP, h, e) for h in range(CHUNKS) for e in range(5))
    for _, h, e in events:
        (products, halve, middle, spread, back_products)[e](h)
        if h == CHUNKS - 1 and e == 3:
            b_second()
    b_copies[7].wait_recv()
    s_send[...] = b_send[1, 8:16] + b_got[7, 8:16]
    sc_copies = [remote(s_send, s_got.at[k], sc_s.at[k], sc_r.at[k], t_peer[k]) for k in range(1, 8)]
    def grad(v, lo, width):
        lows = [lb[h, :, :, :, :, lo:lo + width].reshape(8 * PART, width) for h in range(CHUNKS)]
        rows = [x_part(v, h) for h in range(CHUNKS)]
        return lax.dot_general(
            jnp.concatenate(rows, axis=0), jnp.concatenate(lows, axis=0), (((0,), (0,)), ((), ())),
            preferred_element_type=F32,
        ).astype(BF)

    for lo in range(0, 2 * HALF, 256):
        g_sib[:, lo:lo + 256] = grad(1, lo, 256)
    g_copies = [
        remote(g_sib.at[:, gates], gate_out.at[:, mine], g_s.at[0], g_r.at[0], sib),
        remote(g_sib.at[:, ups], up_out.at[:, mine], g_s.at[1], g_r.at[1], sib),
    ]
    want, have = iota((4 * PART, 4 * PART), 0), iota((4 * PART, 4 * PART), 1)
    source = ((want // 4) % 4) * PART + (want // 16) * 4 + want % 4
    gather = (have == source).astype(BF)
    each = 16 // CHUNKS
    seat = i % each

    def d_copy(h, k):
        there = each * h + xor(seat, k, each.bit_length() - 1)
        return pltpu.make_async_remote_copy(
            src_ref=d_send.at[there], dst_ref=rows_out.at[i],
            send_sem=d_s.at[each * h + k], recv_sem=d_r.at[each * (i // each) + k],
            device_id=(there, j), device_id_type=MESH,
        )

    for h in range(CHUNKS):
        total = z_own[h, pl.ds(j, 1)].reshape(PART, 512).astype(F32)
        for k in far:
            if (h, k) in t_copies:
                t_copies[h, k].wait_recv()
            total = total + t_got[h, k].astype(F32)
        low_rows = (total + cot_rows(j, h) * head_row.astype(F32)).astype(BF)
        stacked = jnp.concatenate([low_rows[:, c:c + 128] for c in range(0, 512, 128)], axis=0)
        d_send[each * h:each * (h + 1)] = dot(gather, stacked).astype(BF).reshape(each, 16, 128)
        for k in range(each - 1, -1, -1):
            if k:
                d_copy(h, k).start()
            else:
                pl.when(i // each != h)(d_copy(h, 0).start)
    rows_out[pl.ds(i, 1)] = d_send[pl.ds(i, 1)]

    for first, out in ((0, gate_out), (HALF, up_out)):
        for lo, width in ((0, 256), (256, 256), (512, 256), (768, 128)):
            where = pl.ds(pl.multiple_of(core * HALF + lo, 128), width)
            out[:, where] = grad(0, first + lo, width)

    score = s_send[...]
    for k in range(1, 8):
        sc_copies[k - 1].wait_recv()
        score = score + s_got[k]
    score = jnp.concatenate([score[r:r + 1] for r in range(4)], axis=1)
    high = score.astype(BF)
    rest = score - high.astype(F32)
    middle = rest.astype(BF)
    last = (rest - middle.astype(F32)).astype(BF)
    split = jnp.concatenate([high, middle, last, jnp.zeros((13, 512), BF)], axis=0)
    moved = dot(split, place[...])
    moved = moved[0:1] + moved[1:2] + moved[2:3]
    score = state["sum"][7:8, 0:ROWS]
    for b in range(8):
        score = score + jnp.where(j == b, moved[:, b * ROWS:(b + 1) * ROWS], 0.0)
    score_out[...] = jnp.zeros_like(score_out)
    score_out[0:1, 0:ROWS] = score
    head_float = head_row.astype(F32)
    for v, tile in ((core, b_send[1]), (1 - core, b_got[7])):
        for c in range(0, HALF, 128):
            column = jnp.broadcast_to(tile[c // 128:c // 128 + 1], (128, 128)).T
            rows = pl.ds(pl.multiple_of(v * HALF + c, 128), 128)
            down_out[rows, :] = (jnp.concatenate([column] * 4, axis=1) * head_float).astype(BF)
    for half in range(CHUNKS):
        for k in range(each):
            got = pltpu.make_async_remote_copy(
                src_ref=d_send.at[0], dst_ref=rows_out.at[each * half + xor(seat, k, each.bit_length() - 1)],
                send_sem=d_s.at[0], recv_sem=d_r.at[each * half + k],
                device_id=sib, device_id_type=MESH,
            )
            if k:
                got.wait_recv()
                d_copy(half, k).wait_send()
            else:
                pl.when(i // each != half)(got.wait_recv)
                pl.when(i // each != half)(d_copy(half, 0).wait_send)
    for copy in g_copies:
        copy.wait_recv()
    for copy in sent:
        copy.wait_send()


def finish_kernel(gate_in, up_in, down_in, score_in, rows_in, gate_out, up_out, down_out, score_out, rows_out, sem):
    copies = [
        pltpu.make_async_copy(gate_in, gate_out, sem.at[0]),
        pltpu.make_async_copy(up_in, up_out, sem.at[1]),
        pltpu.make_async_copy(down_in, down_out, sem.at[2]),
    ]
    for copy in copies:
        copy.start()
    score_out[...] = score_in[0:1, 0:ROWS].reshape(ROWS)
    rows = rows_in[...].astype(F32).reshape(256, 128)
    rows_out[...] = jnp.concatenate([rows[4 * n:4 * n + 4] for n in range(64)], axis=1).astype(BF)
    for copy in copies:
        copy.wait()


def per_device(inputs, ordering, cotangent, gate_weight, up_weight, down_weight, value_head):
    whole = pl.BlockSpec(memory_space=pl.ANY)
    held = pl.BlockSpec(memory_space=pltpu.VMEM)
    dma = pltpu.SemaphoreType.DMA
    cube = (CHUNKS, 2, 2, 2, PART, 2 * HALF)
    gate_grad, up_grad, down_grad, score, rows = pl.pallas_call(
        kernel,
        name="critic",
        out_shape=(
            pltpu.VMEM((512, 2 * HALF), BF),
            pltpu.VMEM((512, 2 * HALF), BF),
            pltpu.VMEM((2 * HALF, 512), BF),
            pltpu.VMEM((8, 128), F32),
            pltpu.VMEM((16, 16, 128), BF),
        ),
        in_specs=[whole] * 7,
        out_specs=(held,) * 5,
        scratch_shapes=[
            pltpu.VMEM((ROWS, 512), BF),
            pltpu.VMEM((512,), jnp.int32),
            pltpu.VMEM((512,), BF),
            pltpu.SMEM((4,), F32),
            pltpu.VMEM((2, 8, ROWS, 512), BF),
            pltpu.VMEM((2, 512, 512), BF),
            pltpu.VMEM((2, 512, 2 * HALF), BF),
            pltpu.VMEM((2 * HALF, 512), BF),
            pltpu.VMEM((512, 512), BF),
            pltpu.VMEM(cube, BF),
            pltpu.VMEM((4, *cube), BF),
            pltpu.VMEM(cube, BF),
            pltpu.VMEM((8, 128), F32),
            pltpu.VMEM((8, 8, 128), F32),
            pltpu.VMEM((3, 16, 128), F32),
            pltpu.VMEM((8, 16, 128), F32),
            pltpu.VMEM((2, 16, 128), F32),
            pltpu.VMEM((8, 16, 128), F32),
            pltpu.VMEM((CHUNKS, 8 * PART, 512), BF),
            pltpu.VMEM((CHUNKS, 8 * PART, 512), BF),
            pltpu.VMEM((CHUNKS, 8, PART, 512), BF),
            pltpu.VMEM((CHUNKS, 8, PART, 512), BF),
            pltpu.VMEM((8, 128), F32),
            pltpu.VMEM((8, 8, 128), F32),
            pltpu.VMEM((512, 2 * HALF), BF),
            pltpu.VMEM((16, 16, 128), BF),
            *[dma((8,))] * 6, dma((2,)), dma((2,)), dma((7,)), dma((12 * CHUNKS,)), dma((12 * CHUNKS,)),
            dma((8,)), dma((8,)), dma((12 * CHUNKS,)), dma((12 * CHUNKS,)), dma((8,)), dma((8,)),
            dma((CHUNKS,)), dma((CHUNKS,)), dma((8 * CHUNKS,)), dma((8 * CHUNKS,)), dma((8,)), dma((8,)), dma((2,)), dma((2,)), dma((16,)), dma((16,)),
        ],
        compiler_params=pltpu.CompilerParams(
            collective_id=0, has_side_effects=True, vmem_limit_bytes=44 * 2**20
        ),
        cost_estimate=pl.CostEstimate(flops=6 * 10**9, bytes_accessed=12 * 10**6, transcendentals=10**5),
    )(*[
        pltpu.with_memory_space_constraint(a, pltpu.HBM)
        for a in (inputs, ordering, value_head, cotangent, gate_weight, up_weight, down_weight)
    ])
    score, rows, gate_grad, up_grad, down_grad = finish_call(gate_grad, up_grad, down_grad, score, rows)
    return (score, rows, gate_grad, up_grad, down_grad)


def finish_call(gate_grad, up_grad, down_grad, score, rows):
    whole = pl.BlockSpec(memory_space=pl.ANY)
    held = pl.BlockSpec(memory_space=pltpu.VMEM)
    outs = pl.pallas_call(
        finish_kernel,
        name="deliver",
        out_shape=(
            jax.ShapeDtypeStruct((512, 2 * HALF), BF),
            jax.ShapeDtypeStruct((512, 2 * HALF), BF),
            jax.ShapeDtypeStruct((2 * HALF, 512), BF),
            jax.ShapeDtypeStruct((ROWS,), F32),
            jax.ShapeDtypeStruct((4, 8192), BF),
        ),
        in_specs=[whole] * 3 + [held] * 2,
        out_specs=(whole,) * 3 + (held,) * 2,
        scratch_shapes=[pltpu.SemaphoreType.DMA((3,))],
        compiler_params=pltpu.CompilerParams(vmem_limit_bytes=8 * 2**20),
    )(gate_grad, up_grad, down_grad, score, rows)
    return outs[3], outs[4], outs[0], outs[1], outs[2]


def solution(mesh):
    placed = (
        P("tensor", "dp"),
        P(),
        P(("dp", "tensor")),
        P("dp", "tensor"),
        P("dp", "tensor"),
        P("tensor", "dp"),
        P("dp"),
    )
    return jax.shard_map(
        per_device,
        mesh=mesh,
        in_specs=placed,
        out_specs=(
            P("tensor"),
            P(("dp", "tensor"), None),
            P("dp", "tensor"),
            P("dp", "tensor"),
            P("tensor", "dp"),
        ),
        check_vma=False,
    )
```
